32 devices in a mesh: lat: 16 (over z, x, core), ma: 2 (over y).
Axes of the slice: x: 2, y: 2, z: 4, core: 2. Of those that a mesh axis runs over, the one named last changes fastest.
Arguments:
- grad_fourier: bfloat16 [4, 1024, 2, 384], P('ma', 'lat'), may hold values from -6 to 6
- legendre: bfloat16 [4, 1024, 640], P('ma', 'lat'), may hold values from -0.1875 to 0.1875
- spectra: bfloat16 [640, 4, 2, 384], P('lat', None, None, 'ma'), may hold values from -3 to 3
- filter_weight: float32 [640, 2, 384], P('lat'), may hold values from -6 to 6
Outputs:
- input_grad: float32 [640, 4, 2, 384], P('lat', 'ma')
- weight_grad: float32 [640, 2, 384], P('lat', None, 'ma')
The draws below stay inside these ranges and needn't reach their ends.
All inputs are finite; a program needn't handle non-finite values.
Results may differ from the reference program's by a relative error of at most 0.0006.
Values may be sent and summed in bfloat16 or wider, within the bound.
A program may use at most 64 MiB of HBM per device.

```python
import jax
import jax.numpy as jnp
from jax import lax

C = 384
L = 640
NLAT = 1024
M = 4


def levels(stream_key, extent, shards, smallest, largest):
    def one(dim, blocks):
        draws = jax.random.uniform(jax.random.fold_in(jax.random.fold_in(stream_key, 6), dim), (blocks,), jnp.float32, smallest / len(shards), largest / len(shards))
        return jnp.repeat(jnp.exp(draws), extent[dim] // blocks).reshape((-1,) + (1,) * (len(extent) - dim - 1))

    loudness = one(*shards[0])
    for cut in shards[1:]:
        loudness = loudness * one(*cut)
    return loudness


def bell_draw(rng, extent, spread, bound, split=(), held_as=jnp.bfloat16):
    entries = spread * jax.random.normal(rng, extent, jnp.float32)
    if split:
        entries = entries * levels(rng, extent, split, -0.22, 0.18)
    return jnp.clip(entries, -bound, bound).astype(held_as)


def setup_inputs(seed: int = 0) -> dict:
    splits = jax.random.split(jax.random.key(seed), 5)
    grad_fourier = bell_draw(splits[0], (M, NLAT, 2, C), 1.0, 6.0, ((0, 2), (1, 16)))
    legendre = bell_draw(splits[1], (M, NLAT, L), NLAT ** -0.5, 0.1875, ((0, 2), (1, 16)))
    spectra = bell_draw(splits[2], (L, M, 2, C), M ** -0.5, 3.0, ((0, 16), (3, 2)))
    filter_weight = bell_draw(splits[3], (L, 2, C), 1.0, 6.0, ((0, 16),), jnp.float32)
    return {"grad_fourier": grad_fourier, "legendre": legendre, "spectra": spectra, "filter_weight": filter_weight}


def reference(grad_fourier, legendre, spectra, filter_weight):
    degrees = jnp.arange(L, dtype=jnp.int32)

    def analyse(order):
        column = lax.dynamic_index_in_dim(legendre, order, 0, keepdims=False)
        table = jnp.where(degrees[None, :] >= order, column, jnp.zeros_like(column))
        rows = lax.dynamic_index_in_dim(grad_fourier, order, 0, keepdims=False)
        flat = rows.reshape(NLAT, 2 * C)
        return jnp.dot(table.T, flat, preferred_element_type=jnp.float32).reshape(L, 2, C)

    stacked = lax.map(analyse, jnp.arange(M, dtype=jnp.int32))
    grads = jnp.transpose(stacked, (1, 0, 2, 3))
    real_grad = grads[:, :, 0, :]
    imag_grad = grads[:, :, 1, :]
    real_weight = filter_weight[:, None, 0, :]
    imag_weight = filter_weight[:, None, 1, :]
    input_grad = jnp.stack([real_weight * real_grad + imag_weight * imag_grad,
                            real_weight * imag_grad - imag_weight * real_grad], axis=2)
    stored = spectra.astype(jnp.float32)
    real_store = stored[:, :, 0, :]
    imag_store = stored[:, :, 1, :]
    weight_grad = jnp.stack([jnp.sum(real_store * real_grad + imag_store * imag_grad, axis=1),
                             jnp.sum(real_store * imag_grad - imag_store * real_grad, axis=1)], axis=1)
    return input_grad, weight_grad
```

```python
import functools

import jax
import jax.numpy as jnp
from jax import lax
from jax.experimental import pallas as pl
from jax.experimental.pallas import tpu as pltpu
from jax.sharding import PartitionSpec as P

MESH = pl.DeviceIdType.MESH
GROUP = 8
CORE, NEAR, FAR = 1, 2, 4


def kernel(sizes, leg_ref, rows_ref, spec_ref, grads_ref, wgrad_ref, tab_send, tab_all, lhs, rows_all, part, part_recv,
           spec_all, wpart, wrecv, tab_ssem, tab_rsem, row_ssem, row_rsem, part_ssem, part_rsem, spec_ssem, spec_rsem,
           w_ssem, w_rsem):
    n, ma, orders, rows, deg, dq, chans = sizes
    blocks = n // GROUP
    chunks = 2 * orders
    width = chans // ma
    lat = lax.axis_index("lat")
    mine = lax.axis_index("ma")
    spot = lax.rem(lat, GROUP)
    block = lax.div(lat, GROUP)
    bits = [lax.rem(lax.div(spot, 1 << b), 2) for b in range(3)]

    def member(slot):
        at = 0
        for b in range(3):
            bit = 1 - bits[b] if slot >> b & 1 else bits[b]
            at = at + bit * (1 << b)
        return at

    def peer(slot):
        return (block * GROUP + member(slot), mine)

    def other_block(step):
        return lax.rem(block + step, blocks)

    def other_ma(step):
        return lax.rem(mine + step, ma)

    barrier = pltpu.get_barrier_semaphore()
    partners = [peer(slot) for slot in range(1, GROUP)]
    partners += [(other_block(step) * GROUP + spot, mine) for step in range(1, blocks)]
    partners += [(lat, other_ma(step)) for step in range(1, ma)]
    for device in partners:
        pl.semaphore_signal(barrier, inc=1, device_id=device, device_id_type=MESH)

    total = leg_ref.shape[2]
    degree = lax.broadcasted_iota(jnp.int32, (orders, rows, total), 2)
    order = lax.broadcasted_iota(jnp.int32, (orders, rows, total), 0) + mine * orders
    table = jnp.where(degree >= order, leg_ref[...].astype(jnp.float32), 0.0)
    turned = table.reshape(orders * rows, total).T
    for at in range(GROUP):
        parts = []
        for b in range(blocks):
            start = (b * GROUP + at) * deg
            part_rows = turned[start:start + deg]
            if dq > deg:
                part_rows = jnp.concatenate([part_rows, jnp.zeros((dq - deg, orders * rows), jnp.float32)], axis=0)
            parts.append(part_rows)
        tab_send[at] = jnp.concatenate(parts, axis=0).astype(jnp.bfloat16)
    pl.semaphore_wait(barrier, len(partners))

    def copy(src, dst, ssem, rsem, device):
        return pltpu.make_async_remote_copy(
            src_ref=src, dst_ref=dst, send_sem=ssem, recv_sem=rsem, device_id=device, device_id_type=MESH)

    tab_copies = {}
    for slot in (FAR, NEAR, FAR + NEAR, FAR + CORE, NEAR + CORE, FAR + NEAR + CORE, CORE):
        tab_copies[slot] = copy(tab_send.at[member(slot)], tab_all.at[slot], tab_ssem.at[slot], tab_rsem.at[slot], peer(slot))
        tab_copies[slot].start()

    row_copies = {}

    def send_rows(k, have, via):
        src = rows_ref.at[k] if have == 0 else rows_all.at[k, have]
        slot = have + via
        row_copies[k, slot] = copy(src, rows_all.at[k, slot], row_ssem.at[k, slot], row_rsem.at[k, slot], peer(via))
        row_copies[k, slot].start()

    def first(k):
        for via in (FAR, NEAR, CORE):
            send_rows(k, 0, via)

    first(0)
    first(1)
    spec_copies = []
    for step in range(1, ma):
        to = other_ma(step)
        spec_copies.append(copy(spec_ref.at[to], spec_all.at[mine], spec_ssem.at[step], spec_rsem.at[step], (lat, to)))
        spec_copies[-1].start()
    for k in range(2, chunks):
        first(k)
    spec_all[mine] = spec_ref[mine]
    for k in range(chunks):
        rows_all[k, 0] = rows_ref[k]

    def spread(k):
        row_copies[k, FAR].wait_recv()
        send_rows(k, FAR, NEAR)
        send_rows(k, FAR, CORE)
        row_copies[k, NEAR].wait_recv()
        send_rows(k, NEAR, CORE)

    def spread_last(k):
        row_copies[k, FAR + NEAR].wait_recv()
        send_rows(k, FAR + NEAR, CORE)

    part_copies = {}

    def multiply(k):
        m = k // 2
        if k == 0:
            for slot in tab_copies:
                tab_copies[slot].wait_recv()
            tabs = [tab_send[spot]] + [tab_all[slot] for slot in range(1, GROUP)]
            for order_at in range(orders):
                lhs[order_at] = jnp.concatenate(
                    [t.astype(jnp.float32)[:, order_at * rows:(order_at + 1) * rows] for t in tabs], axis=1
                ).astype(jnp.bfloat16)
        for slot in (CORE, NEAR + CORE, FAR + CORE, FAR + NEAR + CORE):
            row_copies[k, slot].wait_recv()
        product = jnp.dot(lhs[m], rows_all[k].reshape(GROUP * rows, chans), preferred_element_type=jnp.float32)
        part[k] = product.reshape(blocks, dq, chans)
        for step in range(1, blocks):
            to = other_block(step)
            part_copies[k, step] = copy(part.at[k, to], part_recv.at[k, step], part_ssem.at[k, step], part_rsem.at[k, step],
                                        (to * GROUP + spot, mine))
            part_copies[k, step].start()

    def finish(k):
        value = part[k, block]
        for step in range(1, blocks):
            part_copies[k, step].wait_recv()
            value = value + part_recv[k, step]
        grads_ref[k // 2, k % 2] = value

    def pair(m):
        if m == 0:
            for each in spec_copies:
                each.wait_recv()
        for q in range(ma):
            cut = slice(q * width, (q + 1) * width)
            real_grad = grads_ref[m, 0][:, cut]
            imag_grad = grads_ref[m, 1][:, cut]
            stored = spec_all[q].astype(jnp.float32)
            real_store = stored[2 * m * dq:(2 * m + 1) * dq]
            imag_store = stored[(2 * m + 1) * dq:(2 * m + 2) * dq]
            real = real_store * real_grad + imag_store * imag_grad
            imag = real_store * imag_grad - imag_store * real_grad
            if m == 0:
                wpart[q, 0] = real
                wpart[q, 1] = imag
            else:
                wpart[q, 0] += real
                wpart[q, 1] += imag

    def settle(k):
        finish(k)
        if k % 2:
            pair(k // 2)

    spread(0)
    spread_last(0)
    for k in range(chunks):
        if k + 1 < chunks:
            spread(k + 1)
        multiply(k)
        if k + 1 < chunks:
            spread_last(k + 1)
        if k >= 1:
            settle(k - 1)
    settle(chunks - 1)

    w_copies = []
    for step in range(1, ma):
        to = other_ma(step)
        w_copies.append(copy(wpart.at[to], wrecv.at[step], w_ssem.at[step], w_rsem.at[step], (lat, to)))
        w_copies[-1].start()
    weight = wpart[mine]
    for step in range(1, ma):
        w_copies[step - 1].wait_recv()
        weight = weight + wrecv[step]
    wgrad_ref[...] = weight

    for each in [*tab_copies.values(), *row_copies.values(), *part_copies.values(), *spec_copies, *w_copies]:
        each.wait_send()


def body(n, ma, grad_fourier, legendre, spectra, filter_weight):
    orders, rows, _, chans = grad_fourier.shape
    deg = filter_weight.shape[0]
    dq = -(-deg // 8) * 8
    width = chans // ma
    chunks = 2 * orders
    blocks = n // GROUP
    flat_rows = grad_fourier.transpose(0, 2, 1, 3).reshape(chunks, rows, chans)
    spec = jnp.pad(spectra, ((0, dq - deg), (0, 0), (0, 0), (0, 0))).transpose(1, 2, 0, 3)
    spec = spec.reshape(ma, chunks * dq, width)
    vmem = pl.BlockSpec(memory_space=pltpu.VMEM)
    dma = pltpu.SemaphoreType.DMA
    grads, wgrad = pl.pallas_call(
        functools.partial(kernel, (n, ma, orders, rows, deg, dq, chans)),
        out_shape=(
            jax.ShapeDtypeStruct((orders, 2, dq, chans), jnp.float32),
            jax.ShapeDtypeStruct((2, dq, width), jnp.float32),
        ),
        in_specs=[vmem] * 3,
        out_specs=(vmem, vmem),
        scratch_shapes=[
            pltpu.VMEM((GROUP, blocks * dq, orders * rows), jnp.bfloat16),
            pltpu.VMEM((GROUP, blocks * dq, orders * rows), jnp.bfloat16),
            pltpu.VMEM((orders, blocks * dq, GROUP * rows), jnp.bfloat16),
            pltpu.VMEM((chunks, GROUP, rows, chans), jnp.bfloat16),
            pltpu.VMEM((chunks, blocks, dq, chans), jnp.float32),
            pltpu.VMEM((chunks, blocks, dq, chans), jnp.float32),
            pltpu.VMEM((ma, chunks * dq, width), jnp.bfloat16),
            pltpu.VMEM((ma, 2, dq, width), jnp.float32),
            pltpu.VMEM((ma, 2, dq, width), jnp.float32),
            dma((GROUP,)), dma((GROUP,)),
            dma((chunks, GROUP)), dma((chunks, GROUP)),
            dma((chunks, blocks)), dma((chunks, blocks)),
            dma((ma,)), dma((ma,)),
            dma((ma,)), dma((ma,)),
        ],
        compiler_params=pltpu.CompilerParams(
            collective_id=0, has_side_effects=True, vmem_limit_bytes=24 * 1024 * 1024),
        cost_estimate=pl.CostEstimate(
            flops=2 * chunks * blocks * dq * GROUP * rows * chans, bytes_accessed=4 * chunks * dq * chans, transcendentals=0),
    )(legendre, flat_rows, spec)
    grads = grads[:, :, :deg].transpose(2, 0, 1, 3)
    real_grad = grads[:, :, 0, :]
    imag_grad = grads[:, :, 1, :]
    real_weight = filter_weight[:, None, 0, :]
    imag_weight = filter_weight[:, None, 1, :]
    input_grad = jnp.stack(
        [
            real_weight * real_grad + imag_weight * imag_grad,
            real_weight * imag_grad - imag_weight * real_grad,
        ],
        axis=2,
    )
    return input_grad, wgrad[:, :deg].transpose(1, 0, 2)


def solution(mesh):
    in_specs = (
        P("ma", "lat", None, None),
        P("ma", "lat", None),
        P("lat", None, None, "ma"),
        P("lat", None, None),
    )
    out_specs = (P("lat", "ma", None, None), P("lat", None, "ma"))
    fn = functools.partial(body, mesh.shape["lat"], mesh.shape["ma"])
    return jax.shard_map(fn, mesh=mesh, in_specs=in_specs, out_specs=out_specs, check_vma=False)
```

```python
import functools

import jax
import jax.numpy as jnp
from jax import lax
from jax.experimental import pallas as pl
from jax.experimental.pallas import tpu as pltpu
from jax.sharding import PartitionSpec as P

MESH = pl.DeviceIdType.MESH
GROUP = 8
CORE, NEAR, FAR = 1, 2, 4


def kernel(sizes, leg_hbm, rows_ref, spec_ref, grads_ref, wgrad_ref, leg_ref, tab_send, tab_all, lhs, rows_all, part,
           part_recv, value_all, spec_all, wpart, wrecv, leg_sem, tab_ssem, tab_rsem, row_ssem, row_rsem, part_ssem,
           part_rsem, spec_ssem, spec_rsem, w_ssem, w_rsem):
    n, ma, orders, rows, deg, dq, chans = sizes
    blocks = n // GROUP
    chunks = ma * orders
    width = chans // ma
    lat = lax.axis_index("lat")
    mine = lax.axis_index("ma")
    spot = lax.rem(lat, GROUP)
    block = lax.div(lat, GROUP)
    bits = [lax.rem(lax.div(spot, 1 << b), 2) for b in range(3)]

    def member(slot):
        at = 0
        for b in range(3):
            bit = 1 - bits[b] if slot >> b & 1 else bits[b]
            at = at + bit * (1 << b)
        return at

    def peer(slot):
        return (block * GROUP + member(slot), mine)

    def other_block(step):
        return lax.rem(block + step, blocks)

    def other_ma(step):
        return lax.rem(mine + step, ma)

    barrier = pltpu.get_barrier_semaphore()
    partners = [peer(slot) for slot in range(1, GROUP)]
    partners += [(other_block(step) * GROUP + spot, mine) for step in range(1, blocks)]
    partners += [(lat, other_ma(step)) for step in range(1, ma)]
    for device in partners:
        pl.semaphore_signal(barrier, inc=1, device_id=device, device_id_type=MESH)
    leg_copy = pltpu.make_async_copy(leg_hbm, leg_ref, leg_sem)
    leg_copy.start()

    for q in range(ma):
        place = lax.rem(q - mine - 1 + 2 * ma, ma)
        for m in range(orders):
            cut = slice(q * width, (q + 1) * width)
            rows_all[place * orders + m, 0] = jnp.concatenate(
                [rows_ref[2 * m][:, cut], rows_ref[2 * m + 1][:, cut]], axis=1)
    pl.semaphore_wait(barrier, len(partners))

    def copy(src, dst, ssem, rsem, device):
        return pltpu.make_async_remote_copy(
            src_ref=src, dst_ref=dst, send_sem=ssem, recv_sem=rsem, device_id=device, device_id_type=MESH)

    row_copies = {}

    def send_rows(k, have, via):
        slot = have + via
        row_copies[k, slot] = copy(rows_all.at[k, have], rows_all.at[k, slot], row_ssem.at[k, slot], row_rsem.at[k, slot],
                                   peer(via))
        row_copies[k, slot].start()

    def first(k):
        for via in (FAR, NEAR, CORE):
            send_rows(k, 0, via)

    first(0)

    leg_copy.wait()
    total = leg_ref.shape[2]
    degree = lax.broadcasted_iota(jnp.int32, (orders, rows, total), 2)
    order = lax.broadcasted_iota(jnp.int32, (orders, rows, total), 0) + mine * orders
    table = jnp.where(degree >= order, leg_ref[...].astype(jnp.float32), 0.0)
    turned = table.reshape(orders * rows, total).T
    for at in range(GROUP):
        parts = []
        for b in range(blocks):
            start = (b * GROUP + at) * deg
            part_rows = turned[start:start + deg]
            if dq > deg:
                part_rows = jnp.concatenate([part_rows, jnp.zeros((dq - deg, orders * rows), jnp.float32)], axis=0)
            parts.append(part_rows)
        tab_send[at] = jnp.concatenate(parts, axis=0).astype(jnp.bfloat16)

    tab_copies = {}
    for slot in (FAR, NEAR, FAR + NEAR, FAR + CORE, NEAR + CORE, FAR + NEAR + CORE, CORE):
        tab_copies[slot] = copy(tab_send.at[member(slot)], tab_all.at[slot], tab_ssem.at[slot], tab_rsem.at[slot], peer(slot))
        tab_copies[slot].start()
    spec_copies = []
    for step in range(1, ma):
        to = other_ma(step)
        spec_copies.append(copy(spec_ref.at[to], spec_all.at[mine], spec_ssem.at[step], spec_rsem.at[step], (lat, to)))
        spec_copies[-1].start()
    spec_all[mine] = spec_ref[mine]

    def spread(k):
        row_copies[k, FAR].wait_recv()
        send_rows(k, FAR, NEAR)
        send_rows(k, FAR, CORE)
        if k + 1 < chunks:
            first(k + 1)
        row_copies[k, NEAR].wait_recv()
        send_rows(k, NEAR, CORE)

    def spread_last(k):
        row_copies[k, FAR + NEAR].wait_recv()
        send_rows(k, FAR + NEAR, CORE)

    part_copies = {}

    def multiply(k):
        m = k % orders
        if k == 0:
            for slot in tab_copies:
                tab_copies[slot].wait_recv()
            tabs = [tab_send[spot]] + [tab_all[slot] for slot in range(1, GROUP)]
            for order_at in range(orders):
                lhs[order_at] = jnp.concatenate(
                    [t.astype(jnp.float32)[:, order_at * rows:(order_at + 1) * rows] for t in tabs], axis=1
                ).astype(jnp.bfloat16)
        for slot in (CORE, NEAR + CORE, FAR + CORE, FAR + NEAR + CORE):
            row_copies[k, slot].wait_recv()
        product = jnp.dot(lhs[m], rows_all[k].reshape(GROUP * rows, 2 * width), preferred_element_type=jnp.float32)
        part[k] = product.reshape(blocks, dq, 2 * width)
        for step in range(1, blocks):
            to = other_block(step)
            part_copies[k, step] = copy(part.at[k, to], part_recv.at[k, step], part_ssem.at[k, step], part_rsem.at[k, step],
                                        (to * GROUP + spot, mine))
            part_copies[k, step].start()

    w_copies = []

    def finish(k):
        value = part[k, block]
        for step in range(1, blocks):
            part_copies[k, step].wait_recv()
            value = value + part_recv[k, step]
        step = (k // orders + 1) % ma
        m = k % orders
        q = other_ma(step)
        value_all[q * orders + m] = value
        if k == 0:
            for each in spec_copies:
                each.wait_recv()
        real_grad = value[:, :width]
        imag_grad = value[:, width:]
        stored = spec_all[q].astype(jnp.float32)
        real_store = stored[2 * m * dq:(2 * m + 1) * dq]
        imag_store = stored[(2 * m + 1) * dq:(2 * m + 2) * dq]
        real = real_store * real_grad + imag_store * imag_grad
        imag = real_store * imag_grad - imag_store * real_grad
        if m == 0:
            wpart[step, 0] = real
            wpart[step, 1] = imag
        else:
            wpart[step, 0] += real
            wpart[step, 1] += imag
        if m == orders - 1 and step > 0:
            w_copies.append(copy(wpart.at[step], wrecv.at[step], w_ssem.at[step], w_rsem.at[step], (lat, q)))
            w_copies[-1].start()

    spread(0)
    spread_last(0)
    for k in range(chunks):
        if k + 1 < chunks:
            spread(k + 1)
        multiply(k)
        if k + 1 < chunks:
            spread_last(k + 1)
        if k >= 1:
            finish(k - 1)
    finish(chunks - 1)

    for m in range(orders):
        for r in range(2):
            grads_ref[m, r] = jnp.concatenate(
                [value_all[q * orders + m][:, r * width:(r + 1) * width] for q in range(ma)], axis=1)
    weight = wpart[0]
    for step in range(1, ma):
        w_copies[step - 1].wait_recv()
        weight = weight + wrecv[step]
    wgrad_ref[...] = weight

    for each in [*tab_copies.values(), *row_copies.values(), *part_copies.values(), *spec_copies, *w_copies]:
        each.wait_send()


def body(n, ma, grad_fourier, legendre, spectra, filter_weight):
    orders, rows, _, chans = grad_fourier.shape
    deg = filter_weight.shape[0]
    dq = -(-deg // 8) * 8
    width = chans // ma
    chunks = ma * orders
    blocks = n // GROUP
    flat_rows = grad_fourier.transpose(0, 2, 1, 3).reshape(2 * orders, rows, chans)
    spec = jnp.pad(spectra, ((0, dq - deg), (0, 0), (0, 0), (0, 0))).transpose(1, 2, 0, 3)
    spec = spec.reshape(ma, 2 * orders * dq, width)
    vmem = pl.BlockSpec(memory_space=pltpu.VMEM)
    dma = pltpu.SemaphoreType.DMA
    grads, wgrad = pl.pallas_call(
        functools.partial(kernel, (n, ma, orders, rows, deg, dq, chans)),
        out_shape=(
            jax.ShapeDtypeStruct((orders, 2, dq, chans), jnp.float32),
            jax.ShapeDtypeStruct((2, dq, width), jnp.float32),
        ),
        in_specs=[pl.BlockSpec(memory_space=pltpu.HBM), vmem, vmem],
        out_specs=(vmem, vmem),
        scratch_shapes=[
            pltpu.VMEM(legendre.shape, jnp.bfloat16),
            pltpu.VMEM((GROUP, blocks * dq, orders * rows), jnp.bfloat16),
            pltpu.VMEM((GROUP, blocks * dq, orders * rows), jnp.bfloat16),
            pltpu.VMEM((orders, blocks * dq, GROUP * rows), jnp.bfloat16),
            pltpu.VMEM((chunks, GROUP, rows, 2 * width), jnp.bfloat16),
            pltpu.VMEM((chunks, blocks, dq, 2 * width), jnp.float32),
            pltpu.VMEM((chunks, blocks, dq, 2 * width), jnp.float32),
            pltpu.VMEM((chunks, dq, 2 * width), jnp.float32),
            pltpu.VMEM((ma, 2 * orders * dq, width), jnp.bfloat16),
            pltpu.VMEM((ma, 2, dq, width), jnp.float32),
            pltpu.VMEM((ma, 2, dq, width), jnp.float32),
            dma(()),
            dma((GROUP,)), dma((GROUP,)),
            dma((chunks, GROUP)), dma((chunks, GROUP)),
            dma((chunks, blocks)), dma((chunks, blocks)),
            dma((ma,)), dma((ma,)),
            dma((ma,)), dma((ma,)),
        ],
        compiler_params=pltpu.CompilerParams(
            collective_id=0, has_side_effects=True, vmem_limit_bytes=24 * 1024 * 1024),
        cost_estimate=pl.CostEstimate(
            flops=4 * orders * blocks * dq * GROUP * rows * chans, bytes_accessed=8 * orders * dq * chans, transcendentals=0),
    )(legendre, flat_rows, spec)
    grads = grads[:, :, :deg].transpose(2, 0, 1, 3)
    real_grad = grads[:, :, 0, :]
    imag_grad = grads[:, :, 1, :]
    real_weight = filter_weight[:, None, 0, :]
    imag_weight = filter_weight[:, None, 1, :]
    input_grad = jnp.stack(
        [
            real_weight * real_grad + imag_weight * imag_grad,
            real_weight * imag_grad - imag_weight * real_grad,
        ],
        axis=2,
    )
    return input_grad, wgrad[:, :deg].transpose(1, 0, 2)


def solution(mesh):
    in_specs = (
        P("ma", "lat", None, None),
        P("ma", "lat", None),
        P("lat", None, None, "ma"),
        P("lat", None, None),
    )
    out_specs = (P("lat", "ma", None, None), P("lat", None, "ma"))
    fn = functools.partial(body, mesh.shape["lat"], mesh.shape["ma"])
    return jax.shard_map(fn, mesh=mesh, in_specs=in_specs, out_specs=out_specs, check_vma=False)
```

```python
import functools

import jax
import jax.numpy as jnp
from jax import lax
from jax.experimental import pallas as pl
from jax.experimental.pallas import tpu as pltpu
from jax.sharding import PartitionSpec as P

MESH = pl.DeviceIdType.MESH
GROUP = 8
CORE, NEAR, FAR = 1, 2, 4


def kernel(sizes, leg_hbm, rows_ref, spec_ref, grads_ref, wgrad_ref, leg_ref, tab_send, tab_all, lhs, rows_all, part,
           part_recv, value_all, spec_all, wpart, wrecv, leg_sem, tab_ssem, tab_rsem, row_ssem, row_rsem, part_ssem,
           part_rsem, spec_ssem, spec_rsem, w_ssem, w_rsem):
    n, ma, orders, rows, deg, dq, chans = sizes
    blocks = n // GROUP
    chunks = ma * orders
    width = chans // ma
    lat = lax.axis_index("lat")
    mine = lax.axis_index("ma")
    spot = lax.rem(lat, GROUP)
    block = lax.div(lat, GROUP)
    bits = [lax.rem(lax.div(spot, 1 << b), 2) for b in range(3)]

    def member(slot):
        at = 0
        for b in range(3):
            bit = 1 - bits[b] if slot >> b & 1 else bits[b]
            at = at + bit * (1 << b)
        return at

    def peer(slot):
        return (block * GROUP + member(slot), mine)

    def other_block(step):
        return lax.rem(block + step, blocks)

    def other_ma(step):
        return lax.rem(mine + step, ma)

    barrier = pltpu.get_barrier_semaphore()
    partners = [peer(slot) for slot in range(1, GROUP)]
    partners += [(other_block(step) * GROUP + spot, mine) for step in range(1, blocks)]
    partners += [(lat, other_ma(step)) for step in range(1, ma)]
    for device in partners:
        pl.semaphore_signal(barrier, inc=1, device_id=device, device_id_type=MESH)
    leg_copy = pltpu.make_async_copy(leg_hbm, leg_ref, leg_sem)
    leg_copy.start()

    for q in range(ma):
        place = lax.rem(q - mine - 1 + 2 * ma, ma)
        for m in range(orders):
            cut = slice(q * width, (q + 1) * width)
            rows_all[place * orders + m, 0] = jnp.concatenate(
                [rows_ref[2 * m][:, cut], rows_ref[2 * m + 1][:, cut]], axis=1)
    pl.semaphore_wait(barrier, len(partners))

    def copy(src, dst, ssem, rsem, device):
        return pltpu.make_async_remote_copy(
            src_ref=src, dst_ref=dst, send_sem=ssem, recv_sem=rsem, device_id=device, device_id_type=MESH)

    row_copies = {}

    def send_rows(k, have, via):
        slot = have + via
        row_copies[k, slot] = copy(rows_all.at[k, have], rows_all.at[k, slot], row_ssem.at[k, slot], row_rsem.at[k, slot],
                                   peer(via))
        row_copies[k, slot].start()

    def first(k):
        for via in (FAR, NEAR, CORE):
            send_rows(k, 0, via)

    first(0)

    leg_copy.wait()
    total = leg_ref.shape[2]
    degree = lax.broadcasted_iota(jnp.int32, (orders, rows, total), 2)
    order = lax.broadcasted_iota(jnp.int32, (orders, rows, total), 0) + mine * orders
    table = jnp.where(degree >= order, leg_ref[...].astype(jnp.float32), 0.0)
    turned = table.reshape(orders * rows, total).T
    for at in range(GROUP):
        parts = []
        for b in range(blocks):
            start = (b * GROUP + at) * deg
            part_rows = turned[start:start + deg]
            if dq > deg:
                part_rows = jnp.concatenate([part_rows, jnp.zeros((dq - deg, orders * rows), jnp.float32)], axis=0)
            parts.append(part_rows)
        tab_send[at] = jnp.concatenate(parts, axis=0).astype(jnp.bfloat16)

    tab_copies = {}
    for slot in (FAR, NEAR, FAR + NEAR, FAR + CORE, NEAR + CORE, FAR + NEAR + CORE, CORE):
        tab_copies[slot] = copy(tab_send.at[member(slot)], tab_all.at[slot], tab_ssem.at[slot], tab_rsem.at[slot], peer(slot))
        tab_copies[slot].start()
    spec_copies = []
    for step in range(1, ma):
        to = other_ma(step)
        spec_copies.append(copy(spec_ref.at[to], spec_all.at[mine], spec_ssem.at[step], spec_rsem.at[step], (lat, to)))
        spec_copies[-1].start()
    spec_all[mine] = spec_ref[mine]

    def spread(k):
        row_copies[k, FAR].wait_recv()
        send_rows(k, FAR, NEAR)
        send_rows(k, FAR, CORE)
        if k + 1 < chunks:
            first(k + 1)
        row_copies[k, NEAR].wait_recv()
        send_rows(k, NEAR, CORE)

    def spread_last(k):
        row_copies[k, FAR + NEAR].wait_recv()
        send_rows(k, FAR + NEAR, CORE)

    part_copies = {}

    def multiply(k):
        m = k % orders
        if k == 0:
            for slot in tab_copies:
                tab_copies[slot].wait_recv()
            tabs = [tab_send[spot]] + [tab_all[slot] for slot in range(1, GROUP)]
            for order_at in range(orders):
                lhs[order_at] = jnp.concatenate(
                    [t.astype(jnp.float32)[:, order_at * rows:(order_at + 1) * rows] for t in tabs], axis=1
                ).astype(jnp.bfloat16)
        for slot in (CORE, NEAR + CORE, FAR + CORE, FAR + NEAR + CORE):
            row_copies[k, slot].wait_recv()
        product = jnp.dot(lhs[m], rows_all[k].reshape(GROUP * rows, 2 * width), preferred_element_type=jnp.float32)
        part[k] = product.reshape(blocks, dq, 2 * width)
        for step in range(1, blocks):
            to = other_block(step)
            part_copies[k, step] = copy(part.at[k, to], part_recv.at[k, step], part_ssem.at[k, step], part_rsem.at[k, step],
                                        (to * GROUP + spot, mine))
            part_copies[k, step].start()

    w_copies = []

    def finish(k):
        value = part[k, block]
        for step in range(1, blocks):
            part_copies[k, step].wait_recv()
            value = value + part_recv[k, step]
        step = (k // orders + 1) % ma
        m = k % orders
        q = other_ma(step)
        value_all[q * orders + m] = value
        if k == 0:
            for each in spec_copies:
                each.wait_recv()
        real_grad = value[:, :width]
        imag_grad = value[:, width:]
        stored = spec_all[q].astype(jnp.float32)
        real_store = stored[2 * m * dq:(2 * m + 1) * dq]
        imag_store = stored[(2 * m + 1) * dq:(2 * m + 2) * dq]
        real = real_store * real_grad + imag_store * imag_grad
        imag = real_store * imag_grad - imag_store * real_grad
        if m == 0:
            wpart[step, 0] = real
            wpart[step, 1] = imag
        else:
            wpart[step, 0] += real
            wpart[step, 1] += imag
        if m == orders - 1 and step > 0:
            w_copies.append(copy(wpart.at[step], wrecv.at[step], w_ssem.at[step], w_rsem.at[step], (lat, q)))
            w_copies[-1].start()

    spread(0)
    spread_last(0)
    for k in range(chunks):
        if k + 1 < chunks:
            spread(k + 1)
        multiply(k)
        if k + 1 < chunks:
            spread_last(k + 1)
    for k in range(chunks):
        finish(k)

    for m in range(orders):
        for r in range(2):
            grads_ref[m, r] = jnp.concatenate(
                [value_all[q * orders + m][:, r * width:(r + 1) * width] for q in range(ma)], axis=1)
    weight = wpart[0]
    for step in range(1, ma):
        w_copies[step - 1].wait_recv()
        weight = weight + wrecv[step]
    wgrad_ref[...] = weight

    for each in [*tab_copies.values(), *row_copies.values(), *part_copies.values(), *spec_copies, *w_copies]:
        each.wait_send()


def body(n, ma, grad_fourier, legendre, spectra, filter_weight):
    orders, rows, _, chans = grad_fourier.shape
    deg = filter_weight.shape[0]
    dq = -(-deg // 8) * 8
    width = chans // ma
    chunks = ma * orders
    blocks = n // GROUP
    flat_rows = grad_fourier.transpose(0, 2, 1, 3).reshape(2 * orders, rows, chans)
    spec = jnp.pad(spectra, ((0, dq - deg), (0, 0), (0, 0), (0, 0))).transpose(1, 2, 0, 3)
    spec = spec.reshape(ma, 2 * orders * dq, width)
    vmem = pl.BlockSpec(memory_space=pltpu.VMEM)
    dma = pltpu.SemaphoreType.DMA
    grads, wgrad = pl.pallas_call(
        functools.partial(kernel, (n, ma, orders, rows, deg, dq, chans)),
        out_shape=(
            jax.ShapeDtypeStruct((orders, 2, dq, chans), jnp.float32),
            jax.ShapeDtypeStruct((2, dq, width), jnp.float32),
        ),
        in_specs=[pl.BlockSpec(memory_space=pltpu.HBM), vmem, vmem],
        out_specs=(vmem, vmem),
        scratch_shapes=[
            pltpu.VMEM(legendre.shape, jnp.bfloat16),
            pltpu.VMEM((GROUP, blocks * dq, orders * rows), jnp.bfloat16),
            pltpu.VMEM((GROUP, blocks * dq, orders * rows), jnp.bfloat16),
            pltpu.VMEM((orders, blocks * dq, GROUP * rows), jnp.bfloat16),
            pltpu.VMEM((chunks, GROUP, rows, 2 * width), jnp.bfloat16),
            pltpu.VMEM((chunks, blocks, dq, 2 * width), jnp.float32),
            pltpu.VMEM((chunks, blocks, dq, 2 * width), jnp.float32),
            pltpu.VMEM((chunks, dq, 2 * width), jnp.float32),
            pltpu.VMEM((ma, 2 * orders * dq, width), jnp.bfloat16),
            pltpu.VMEM((ma, 2, dq, width), jnp.float32),
            pltpu.VMEM((ma, 2, dq, width), jnp.float32),
            dma(()),
            dma((GROUP,)), dma((GROUP,)),
            dma((chunks, GROUP)), dma((chunks, GROUP)),
            dma((chunks, blocks)), dma((chunks, blocks)),
            dma((ma,)), dma((ma,)),
            dma((ma,)), dma((ma,)),
        ],
        compiler_params=pltpu.CompilerParams(
            collective_id=0, has_side_effects=True, vmem_limit_bytes=24 * 1024 * 1024),
        cost_estimate=pl.CostEstimate(
            flops=4 * orders * blocks * dq * GROUP * rows * chans, bytes_accessed=8 * orders * dq * chans, transcendentals=0),
    )(legendre, flat_rows, spec)
    grads = grads[:, :, :deg].transpose(2, 0, 1, 3)
    real_grad = grads[:, :, 0, :]
    imag_grad = grads[:, :, 1, :]
    real_weight = filter_weight[:, None, 0, :]
    imag_weight = filter_weight[:, None, 1, :]
    input_grad = jnp.stack(
        [
            real_weight * real_grad + imag_weight * imag_grad,
            real_weight * imag_grad - imag_weight * real_grad,
        ],
        axis=2,
    )
    return input_grad, wgrad[:, :deg].transpose(1, 0, 2)


def solution(mesh):
    in_specs = (
        P("ma", "lat", None, None),
        P("ma", "lat", None),
        P("lat", None, None, "ma"),
        P("lat", None, None),
    )
    out_specs = (P("lat", "ma", None, None), P("lat", None, "ma"))
    fn = functools.partial(body, mesh.shape["lat"], mesh.shape["ma"])
    return jax.shard_map(fn, mesh=mesh, in_specs=in_specs, out_specs=out_specs, check_vma=False)
```

```python
import functools

import jax
import jax.numpy as jnp
from jax import lax
from jax.experimental import pallas as pl
from jax.experimental.pallas import tpu as pltpu
from jax.sharding import PartitionSpec as P

MESH = pl.DeviceIdType.MESH
GROUP = 8
CORE, NEAR, FAR = 1, 2, 4


def kernel(sizes, grad_hbm, leg_hbm, spec_hbm, filter_hbm, input_ref, wgrad_ref, grad_ref, leg_ref, raw_ref, filter_ref,
           tab_send, tab_all, lhs, rows_all, part, part_recv, value_all, spec_send, spec_all, wpart, wrecv, in_sem, tab_ssem,
           tab_rsem, row_ssem, row_rsem, part_ssem, part_rsem, spec_ssem, spec_rsem, w_ssem, w_rsem):
    n, ma, orders, rows, deg, dq, chans = sizes
    blocks = n // GROUP
    chunks = ma * orders
    width = chans // ma
    lat = lax.axis_index("lat")
    mine = lax.axis_index("ma")
    spot = lax.rem(lat, GROUP)
    block = lax.div(lat, GROUP)
    bits = [lax.rem(lax.div(spot, 1 << b), 2) for b in range(3)]

    def member(slot):
        at = 0
        for b in range(3):
            bit = 1 - bits[b] if slot >> b & 1 else bits[b]
            at = at + bit * (1 << b)
        return at

    def peer(slot):
        return (block * GROUP + member(slot), mine)

    def other_block(step):
        return lax.rem(block + step, blocks)

    def other_ma(step):
        return lax.rem(mine + step, ma)

    barrier = pltpu.get_barrier_semaphore()
    partners = [peer(slot) for slot in range(1, GROUP)]
    partners += [(other_block(step) * GROUP + spot, mine) for step in range(1, blocks)]
    partners += [(lat, other_ma(step)) for step in range(1, ma)]
    for device in partners:
        pl.semaphore_signal(barrier, inc=1, device_id=device, device_id_type=MESH)
    loads = []
    for at, (far, near) in enumerate(((grad_hbm, grad_ref), (leg_hbm, leg_ref), (spec_hbm, raw_ref), (filter_hbm, filter_ref))):
        loads.append(pltpu.make_async_copy(far, near, in_sem.at[at]))
        loads[-1].start()

    def stage(m):
        halves = grad_ref[m].astype(jnp.float32)
        halves = [halves[:, r, :].astype(jnp.bfloat16) for r in range(2)]
        for q in range(ma):
            place = lax.rem(q - mine - 1 + 2 * ma, ma)
            cut = slice(q * width, (q + 1) * width)
            rows_all[place * orders + m, 0] = jnp.concatenate([half[:, cut] for half in halves], axis=1)

    loads[0].wait()
    stage(0)
    pl.semaphore_wait(barrier, len(partners))

    def copy(src, dst, ssem, rsem, device):
        return pltpu.make_async_remote_copy(
            src_ref=src, dst_ref=dst, send_sem=ssem, recv_sem=rsem, device_id=device, device_id_type=MESH)

    row_copies = {}

    def send_rows(k, have, via):
        slot = have + via
        row_copies[k, slot] = copy(rows_all.at[k, have], rows_all.at[k, slot], row_ssem.at[k, slot], row_rsem.at[k, slot],
                                   peer(via))
        row_copies[k, slot].start()

    def first(k):
        for via in (FAR, NEAR, CORE):
            send_rows(k, 0, via)

    first(0)

    loads[1].wait()
    total = leg_ref.shape[2]
    degree = lax.broadcasted_iota(jnp.int32, (orders, rows, total), 2)
    order = lax.broadcasted_iota(jnp.int32, (orders, rows, total), 0) + mine * orders
    table = jnp.where(degree >= order, leg_ref[...].astype(jnp.float32), 0.0)
    turned = table.reshape(orders * rows, total).T
    for at in range(GROUP):
        parts = []
        for b in range(blocks):
            start = (b * GROUP + at) * deg
            part_rows = turned[start:start + deg]
            if dq > deg:
                part_rows = jnp.concatenate([part_rows, jnp.zeros((dq - deg, orders * rows), jnp.float32)], axis=0)
            parts.append(part_rows)
        tab_send[at] = jnp.concatenate(parts, axis=0).astype(jnp.bfloat16)

    tab_copies = {}
    for slot in (FAR, NEAR, FAR + NEAR, FAR + CORE, NEAR + CORE, FAR + NEAR + CORE, CORE):
        tab_copies[slot] = copy(tab_send.at[member(slot)], tab_all.at[slot], tab_ssem.at[slot], tab_rsem.at[slot], peer(slot))
        tab_copies[slot].start()
    for m in range(1, orders):
        stage(m)
    spec_copies = []

    def send_spectra():
        loads[2].wait()
        raw = raw_ref[...].astype(jnp.float32)
        for q in range(ma):
            parts = []
            for m in range(orders):
                for r in range(2):
                    parts.append(raw[:, q * orders + m, r, :])
                    if dq > deg:
                        parts.append(jnp.zeros((dq - deg, width), jnp.float32))
            spec_send[q] = jnp.concatenate(parts, axis=0).astype(jnp.bfloat16)
        for step in range(1, ma):
            to = other_ma(step)
            spec_copies.append(copy(spec_send.at[to], spec_all.at[mine], spec_ssem.at[step], spec_rsem.at[step], (lat, to)))
            spec_copies[-1].start()
        spec_all[mine] = spec_send[mine]

    def spread(k):
        row_copies[k, FAR].wait_recv()
        send_rows(k, FAR, NEAR)
        send_rows(k, FAR, CORE)
        if k + 1 < chunks:
            first(k + 1)
        row_copies[k, NEAR].wait_recv()
        send_rows(k, NEAR, CORE)

    def spread_last(k):
        row_copies[k, FAR + NEAR].wait_recv()
        send_rows(k, FAR + NEAR, CORE)

    part_copies = {}

    def multiply(k):
        m = k % orders
        if k == 0:
            for slot in tab_copies:
                tab_copies[slot].wait_recv()
            tabs = [tab_send[spot]] + [tab_all[slot] for slot in range(1, GROUP)]
            for order_at in range(orders):
                lhs[order_at] = jnp.concatenate(
                    [t.astype(jnp.float32)[:, order_at * rows:(order_at + 1) * rows] for t in tabs], axis=1
                ).astype(jnp.bfloat16)
        for slot in (CORE, NEAR + CORE, FAR + CORE, FAR + NEAR + CORE):
            row_copies[k, slot].wait_recv()
        product = jnp.dot(lhs[m], rows_all[k].reshape(GROUP * rows, 2 * width), preferred_element_type=jnp.float32)
        part[k] = product.reshape(blocks, dq, 2 * width)
        for step in range(1, blocks):
            to = other_block(step)
            part_copies[k, step] = copy(part.at[k, to], part_recv.at[k, step], part_ssem.at[k, step], part_rsem.at[k, step],
                                        (to * GROUP + spot, mine))
            part_copies[k, step].start()

    w_copies = []

    def finish(k):
        value = part[k, block]
        for step in range(1, blocks):
            part_copies[k, step].wait_recv()
            value = value + part_recv[k, step]
        step = (k // orders + 1) % ma
        m = k % orders
        q = other_ma(step)
        value_all[q * orders + m] = value
        if k == 0:
            for each in spec_copies:
                each.wait_recv()
        real_grad = value[:, :width]
        imag_grad = value[:, width:]
        stored = spec_all[q].astype(jnp.float32)
        real_store = stored[2 * m * dq:(2 * m + 1) * dq]
        imag_store = stored[(2 * m + 1) * dq:(2 * m + 2) * dq]
        real = real_store * real_grad + imag_store * imag_grad
        imag = real_store * imag_grad - imag_store * real_grad
        if m == 0:
            wpart[step, 0] = real
            wpart[step, 1] = imag
        else:
            wpart[step, 0] += real
            wpart[step, 1] += imag
        if m == orders - 1 and step > 0:
            w_copies.append(copy(wpart.at[step], wrecv.at[step], w_ssem.at[step], w_rsem.at[step], (lat, q)))
            w_copies[-1].start()

    spread(0)
    spread_last(0)
    for k in range(chunks):
        if k + 1 < chunks:
            spread(k + 1)
        multiply(k)
        if k == 0:
            send_spectra()
        if k + 1 < chunks:
            spread_last(k + 1)

    loads[3].wait()
    real_weight, imag_weight = [filter_ref[:, r, :] for r in range(2)]
    for k in range(chunks):
        finish(k)
        if k >= chunks - orders:
            m = k % orders
            real_grad, imag_grad = [
                jnp.concatenate([value_all[q * orders + m][:deg, r * width:(r + 1) * width] for q in range(ma)], axis=1)
                for r in range(2)]
            input_ref[:, m, 0, :] = real_weight * real_grad + imag_weight * imag_grad
            input_ref[:, m, 1, :] = real_weight * imag_grad - imag_weight * real_grad
    weight = wpart[0]
    for step in range(1, ma):
        w_copies[step - 1].wait_recv()
        weight = weight + wrecv[step]
    for r in range(2):
        wgrad_ref[:, r, :] = weight[r, :deg]

    for each in [*tab_copies.values(), *row_copies.values(), *part_copies.values(), *spec_copies, *w_copies]:
        each.wait_send()


def body(n, ma, grad_fourier, legendre, spectra, filter_weight):
    orders, rows, _, chans = grad_fourier.shape
    deg = filter_weight.shape[0]
    dq = -(-deg // 8) * 8
    width = chans // ma
    chunks = ma * orders
    blocks = n // GROUP
    vmem = pl.BlockSpec(memory_space=pltpu.VMEM)
    dma = pltpu.SemaphoreType.DMA
    return pl.pallas_call(
        functools.partial(kernel, (n, ma, orders, rows, deg, dq, chans)),
        out_shape=(
            jax.ShapeDtypeStruct((deg, orders, 2, chans), jnp.float32),
            jax.ShapeDtypeStruct((deg, 2, width), jnp.float32),
        ),
        in_specs=[pl.BlockSpec(memory_space=pltpu.HBM)] * 4,
        out_specs=(vmem, vmem),
        scratch_shapes=[
            pltpu.VMEM(grad_fourier.shape, jnp.bfloat16),
            pltpu.VMEM(legendre.shape, jnp.bfloat16),
            pltpu.VMEM(spectra.shape, jnp.bfloat16),
            pltpu.VMEM(filter_weight.shape, jnp.float32),
            pltpu.VMEM((GROUP, blocks * dq, orders * rows), jnp.bfloat16),
            pltpu.VMEM((GROUP, blocks * dq, orders * rows), jnp.bfloat16),
            pltpu.VMEM((orders, blocks * dq, GROUP * rows), jnp.bfloat16),
            pltpu.VMEM((chunks, GROUP, rows, 2 * width), jnp.bfloat16),
            pltpu.VMEM((chunks, blocks, dq, 2 * width), jnp.float32),
            pltpu.VMEM((chunks, blocks, dq, 2 * width), jnp.float32),
            pltpu.VMEM((chunks, dq, 2 * width), jnp.float32),
            pltpu.VMEM((ma, 2 * orders * dq, width), jnp.bfloat16),
            pltpu.VMEM((ma, 2 * orders * dq, width), jnp.bfloat16),
            pltpu.VMEM((ma, 2, dq, width), jnp.float32),
            pltpu.VMEM((ma, 2, dq, width), jnp.float32),
            dma((4,)),
            dma((GROUP,)), dma((GROUP,)),
            dma((chunks, GROUP)), dma((chunks, GROUP)),
            dma((chunks, blocks)), dma((chunks, blocks)),
            dma((ma,)), dma((ma,)),
            dma((ma,)), dma((ma,)),
        ],
        compiler_params=pltpu.CompilerParams(
            collective_id=0, has_side_effects=True, vmem_limit_bytes=60 * 1024 * 1024),
        cost_estimate=pl.CostEstimate(
            flops=4 * orders * blocks * dq * GROUP * rows * chans, bytes_accessed=8 * orders * dq * chans, transcendentals=0),
    )(grad_fourier, legendre, spectra, filter_weight)


def solution(mesh):
    in_specs = (
        P("ma", "lat", None, None),
        P("ma", "lat", None),
        P("lat", None, None, "ma"),
        P("lat", None, None),
    )
    out_specs = (P("lat", "ma", None, None), P("lat", None, "ma"))
    fn = functools.partial(body, mesh.shape["lat"], mesh.shape["ma"])
    return jax.shard_map(fn, mesh=mesh, in_specs=in_specs, out_specs=out_specs, check_vma=False)
```

```python
import functools

import jax
import jax.numpy as jnp
from jax import lax
from jax.experimental import pallas as pl
from jax.experimental.pallas import tpu as pltpu
from jax.sharding import PartitionSpec as P

MESH = pl.DeviceIdType.MESH
GROUP = 8
CORE, NEAR, FAR = 1, 2, 4


def kernel(sizes, grad_hbm, leg_hbm, spec_hbm, filter_hbm, input_ref, wgrad_ref, grad_ref, leg_ref, raw_ref, filter_ref,
           tab_send, tab_all, lhs, rows_all, part, part_recv, value_all, spec_send, spec_all, wpart, wrecv, in_sem, tab_ssem,
           tab_rsem, row_ssem, row_rsem, part_ssem, part_rsem, spec_ssem, spec_rsem, w_ssem, w_rsem):
    n, ma, orders, rows, deg, dq, chans = sizes
    blocks = n // GROUP
    chunks = ma * orders
    width = chans // ma
    lat = lax.axis_index("lat")
    mine = lax.axis_index("ma")
    spot = lax.rem(lat, GROUP)
    block = lax.div(lat, GROUP)
    bits = [lax.rem(lax.div(spot, 1 << b), 2) for b in range(3)]

    def member(slot):
        at = 0
        for b in range(3):
            bit = 1 - bits[b] if slot >> b & 1 else bits[b]
            at = at + bit * (1 << b)
        return at

    def peer(slot):
        return (block * GROUP + member(slot), mine)

    def other_block(step):
        return lax.rem(block + step, blocks)

    def other_ma(step):
        return lax.rem(mine + step, ma)

    barrier = pltpu.get_barrier_semaphore()
    partners = [peer(slot) for slot in range(1, GROUP)]
    partners += [(other_block(step) * GROUP + spot, mine) for step in range(1, blocks)]
    partners += [(lat, other_ma(step)) for step in range(1, ma)]
    for device in partners:
        pl.semaphore_signal(barrier, inc=1, device_id=device, device_id_type=MESH)
    loads = []
    for at, (far, near) in enumerate(((grad_hbm, grad_ref), (leg_hbm, leg_ref), (spec_hbm, raw_ref), (filter_hbm, filter_ref))):
        loads.append(pltpu.make_async_copy(far, near, in_sem.at[at]))
        loads[-1].start()

    def stage(m):
        halves = grad_ref[m].astype(jnp.float32)
        halves = [halves[:, r, :].astype(jnp.bfloat16) for r in range(2)]
        for q in range(ma):
            place = lax.rem(q - mine - 1 + 2 * ma, ma)
            cut = slice(q * width, (q + 1) * width)
            rows_all[place * orders + m, 0] = jnp.concatenate([half[:, cut] for half in halves], axis=1)

    loads[0].wait()
    stage(0)
    pl.semaphore_wait(barrier, len(partners))

    def copy(src, dst, ssem, rsem, device):
        return pltpu.make_async_remote_copy(
            src_ref=src, dst_ref=dst, send_sem=ssem, recv_sem=rsem, device_id=device, device_id_type=MESH)

    row_copies = {}

    def send_rows(k, have, via):
        slot = have + via
        row_copies[k, slot] = copy(rows_all.at[k, have], rows_all.at[k, slot], row_ssem.at[k, slot], row_rsem.at[k, slot],
                                   peer(via))
        row_copies[k, slot].start()

    def first(k):
        for via in (FAR, NEAR, CORE):
            send_rows(k, 0, via)

    first(0)

    loads[1].wait()
    total = leg_ref.shape[2]
    degree = lax.broadcasted_iota(jnp.int32, (orders, rows, total), 2)
    order = lax.broadcasted_iota(jnp.int32, (orders, rows, total), 0) + mine * orders
    table = jnp.where(degree >= order, leg_ref[...].astype(jnp.float32), 0.0)
    turned = table.reshape(orders * rows, total).T
    for at in range(GROUP):
        parts = []
        for b in range(blocks):
            start = (b * GROUP + at) * deg
            part_rows = turned[start:start + deg]
            if dq > deg:
                part_rows = jnp.concatenate([part_rows, jnp.zeros((dq - deg, orders * rows), jnp.float32)], axis=0)
            parts.append(part_rows)
        tab_send[at] = jnp.concatenate(parts, axis=0).astype(jnp.bfloat16)

    tab_copies = {}
    for slot in (FAR, NEAR, FAR + NEAR, FAR + CORE, NEAR + CORE, FAR + NEAR + CORE, CORE):
        tab_copies[slot] = copy(tab_send.at[member(slot)], tab_all.at[slot], tab_ssem.at[slot], tab_rsem.at[slot], peer(slot))
        tab_copies[slot].start()
    for m in range(1, orders):
        stage(m)
    spec_copies = []

    def send_spectra():
        loads[2].wait()
        raw = raw_ref[...].astype(jnp.float32)
        for q in range(ma):
            parts = []
            for m in range(orders):
                for r in range(2):
                    parts.append(raw[:, q * orders + m, r, :])
                    if dq > deg:
                        parts.append(jnp.zeros((dq - deg, width), jnp.float32))
            spec_send[q] = jnp.concatenate(parts, axis=0).astype(jnp.bfloat16)
        for step in range(1, ma):
            to = other_ma(step)
            spec_copies.append(copy(spec_send.at[to], spec_all.at[mine], spec_ssem.at[step], spec_rsem.at[step], (lat, to)))
            spec_copies[-1].start()
        spec_all[mine] = spec_send[mine]

    def spread(k):
        early, late = (NEAR, FAR) if k % 2 else (FAR, NEAR)
        row_copies[k, early].wait_recv()
        send_rows(k, early, late)
        send_rows(k, early, CORE)
        if k + 1 < chunks:
            first(k + 1)
        row_copies[k, late].wait_recv()
        send_rows(k, late, CORE)

    def spread_last(k):
        row_copies[k, FAR + NEAR].wait_recv()
        send_rows(k, FAR + NEAR, CORE)

    part_copies = {}

    def multiply(k):
        m = k % orders
        if k == 0:
            for slot in tab_copies:
                tab_copies[slot].wait_recv()
            tabs = [tab_send[spot]] + [tab_all[slot] for slot in range(1, GROUP)]
            for order_at in range(orders):
                lhs[order_at] = jnp.concatenate(
                    [t.astype(jnp.float32)[:, order_at * rows:(order_at + 1) * rows] for t in tabs], axis=1
                ).astype(jnp.bfloat16)
        for slot in (CORE, NEAR + CORE, FAR + CORE, FAR + NEAR + CORE):
            row_copies[k, slot].wait_recv()
        product = jnp.dot(lhs[m], rows_all[k].reshape(GROUP * rows, 2 * width), preferred_element_type=jnp.float32)
        part[k] = product.reshape(blocks, dq, 2 * width)
        for step in range(1, blocks):
            to = other_block(step)
            part_copies[k, step] = copy(part.at[k, to], part_recv.at[k, step], part_ssem.at[k, step], part_rsem.at[k, step],
                                        (to * GROUP + spot, mine))
            part_copies[k, step].start()

    w_copies = []

    def finish(k):
        value = part[k, block]
        for step in range(1, blocks):
            part_copies[k, step].wait_recv()
            value = value + part_recv[k, step]
        step = (k // orders + 1) % ma
        m = k % orders
        q = other_ma(step)
        value_all[q * orders + m] = value
        if k == 0:
            for each in spec_copies:
                each.wait_recv()
        real_grad = value[:, :width]
        imag_grad = value[:, width:]
        stored = spec_all[q].astype(jnp.float32)
        real_store = stored[2 * m * dq:(2 * m + 1) * dq]
        imag_store = stored[(2 * m + 1) * dq:(2 * m + 2) * dq]
        real = real_store * real_grad + imag_store * imag_grad
        imag = real_store * imag_grad - imag_store * real_grad
        if m == 0:
            wpart[step, 0] = real
            wpart[step, 1] = imag
        else:
            wpart[step, 0] += real
            wpart[step, 1] += imag
        if m == orders - 1 and step > 0:
            w_copies.append(copy(wpart.at[step], wrecv.at[step], w_ssem.at[step], w_rsem.at[step], (lat, q)))
            w_copies[-1].start()

    spread(0)
    spread_last(0)
    for k in range(chunks):
        if k + 1 < chunks:
            spread(k + 1)
        multiply(k)
        if k == 0:
            send_spectra()
        if k + 1 < chunks:
            spread_last(k + 1)

    loads[3].wait()
    real_weight, imag_weight = [filter_ref[:, r, :] for r in range(2)]
    for k in range(chunks):
        finish(k)
        if k >= chunks - orders:
            m = k % orders
            real_grad, imag_grad = [
                jnp.concatenate([value_all[q * orders + m][:deg, r * width:(r + 1) * width] for q in range(ma)], axis=1)
                for r in range(2)]
            input_ref[:, m, 0, :] = real_weight * real_grad + imag_weight * imag_grad
            input_ref[:, m, 1, :] = real_weight * imag_grad - imag_weight * real_grad
    weight = wpart[0]
    for step in range(1, ma):
        w_copies[step - 1].wait_recv()
        weight = weight + wrecv[step]
    for r in range(2):
        wgrad_ref[:, r, :] = weight[r, :deg]

    for each in [*tab_copies.values(), *row_copies.values(), *part_copies.values(), *spec_copies, *w_copies]:
        each.wait_send()


def write_out(input_ref, wgrad_ref, input_out, wgrad_out, sem):
    copies = [
        pltpu.make_async_copy(input_ref, input_out, sem.at[0]),
        pltpu.make_async_copy(wgrad_ref, wgrad_out, sem.at[1]),
    ]
    for each in copies:
        each.start()
    for each in copies:
        each.wait()


def body(n, ma, grad_fourier, legendre, spectra, filter_weight):
    orders, rows, _, chans = grad_fourier.shape
    deg = filter_weight.shape[0]
    dq = -(-deg // 8) * 8
    width = chans // ma
    chunks = ma * orders
    blocks = n // GROUP
    vmem = pl.BlockSpec(memory_space=pltpu.VMEM)
    dma = pltpu.SemaphoreType.DMA
    input_grad, wgrad = pl.pallas_call(
        functools.partial(kernel, (n, ma, orders, rows, deg, dq, chans)),
        out_shape=(
            jax.ShapeDtypeStruct((deg, orders, 2, chans), jnp.float32),
            jax.ShapeDtypeStruct((deg, 2, width), jnp.float32),
        ),
        in_specs=[pl.BlockSpec(memory_space=pltpu.HBM)] * 4,
        out_specs=(vmem, vmem),
        scratch_shapes=[
            pltpu.VMEM(grad_fourier.shape, jnp.bfloat16),
            pltpu.VMEM(legendre.shape, jnp.bfloat16),
            pltpu.VMEM(spectra.shape, jnp.bfloat16),
            pltpu.VMEM(filter_weight.shape, jnp.float32),
            pltpu.VMEM((GROUP, blocks * dq, orders * rows), jnp.bfloat16),
            pltpu.VMEM((GROUP, blocks * dq, orders * rows), jnp.bfloat16),
            pltpu.VMEM((orders, blocks * dq, GROUP * rows), jnp.bfloat16),
            pltpu.VMEM((chunks, GROUP, rows, 2 * width), jnp.bfloat16),
            pltpu.VMEM((chunks, blocks, dq, 2 * width), jnp.float32),
            pltpu.VMEM((chunks, blocks, dq, 2 * width), jnp.float32),
            pltpu.VMEM((chunks, dq, 2 * width), jnp.float32),
            pltpu.VMEM((ma, 2 * orders * dq, width), jnp.bfloat16),
            pltpu.VMEM((ma, 2 * orders * dq, width), jnp.bfloat16),
            pltpu.VMEM((ma, 2, dq, width), jnp.float32),
            pltpu.VMEM((ma, 2, dq, width), jnp.float32),
            dma((4,)),
            dma((GROUP,)), dma((GROUP,)),
            dma((chunks, GROUP)), dma((chunks, GROUP)),
            dma((chunks, blocks)), dma((chunks, blocks)),
            dma((ma,)), dma((ma,)),
            dma((ma,)), dma((ma,)),
        ],
        compiler_params=pltpu.CompilerParams(
            collective_id=0, has_side_effects=True, vmem_limit_bytes=60 * 1024 * 1024),
        cost_estimate=pl.CostEstimate(
            flops=4 * orders * blocks * dq * GROUP * rows * chans, bytes_accessed=8 * orders * dq * chans, transcendentals=0),
    )(grad_fourier, legendre, spectra, filter_weight)
    hbm = pl.BlockSpec(memory_space=pltpu.HBM)
    return pl.pallas_call(
        write_out,
        out_shape=(
            jax.ShapeDtypeStruct(input_grad.shape, jnp.float32),
            jax.ShapeDtypeStruct(wgrad.shape, jnp.float32),
        ),
        in_specs=[hbm] * 2,
        out_specs=(hbm, hbm),
        scratch_shapes=[dma((2,))],
        compiler_params=pltpu.CompilerParams(vmem_limit_bytes=60 * 1024 * 1024),
    )(input_grad, wgrad)


def solution(mesh):
    in_specs = (
        P("ma", "lat", None, None),
        P("ma", "lat", None),
        P("lat", None, None, "ma"),
        P("lat", None, None),
    )
    out_specs = (P("lat", "ma", None, None), P("lat", None, "ma"))
    fn = functools.partial(body, mesh.shape["lat"], mesh.shape["ma"])
    return jax.shard_map(fn, mesh=mesh, in_specs=in_specs, out_specs=out_specs, check_vma=False)
```

```python
import functools

import jax
import jax.numpy as jnp
from jax import lax
from jax.experimental import pallas as pl
from jax.experimental.pallas import tpu as pltpu
from jax.sharding import PartitionSpec as P

MESH = pl.DeviceIdType.MESH
GROUP = 8
CORE, NEAR, FAR = 1, 2, 4


def kernel(sizes, leg_hbm, rows_ref, spec_ref, grads_ref, wgrad_ref, leg_ref, tab_send, tab_all, lhs, rows_all, part,
           part_recv, value_all, spec_all, wpart, wrecv, leg_sem, tab_ssem, tab_rsem, row_ssem, row_rsem, part_ssem,
           part_rsem, spec_ssem, spec_rsem, w_ssem, w_rsem):
    n, ma, orders, rows, deg, dq, chans = sizes
    blocks = n // GROUP
    chunks = ma * orders
    width = chans // ma
    lat = lax.axis_index("lat")
    mine = lax.axis_index("ma")
    spot = lax.rem(lat, GROUP)
    block = lax.div(lat, GROUP)
    bits = [lax.rem(lax.div(spot, 1 << b), 2) for b in range(3)]

    def member(slot):
        at = 0
        for b in range(3):
            bit = 1 - bits[b] if slot >> b & 1 else bits[b]
            at = at + bit * (1 << b)
        return at

    def peer(slot):
        return (block * GROUP + member(slot), mine)

    def other_block(step):
        return lax.rem(block + step, blocks)

    def other_ma(step):
        return lax.rem(mine + step, ma)

    barrier = pltpu.get_barrier_semaphore()
    partners = [peer(slot) for slot in range(1, GROUP)]
    partners += [(other_block(step) * GROUP + spot, mine) for step in range(1, blocks)]
    partners += [(lat, other_ma(step)) for step in range(1, ma)]
    for device in partners:
        pl.semaphore_signal(barrier, inc=1, device_id=device, device_id_type=MESH)
    leg_copy = pltpu.make_async_copy(leg_hbm, leg_ref, leg_sem)
    leg_copy.start()

    for q in range(ma):
        place = lax.rem(q - mine - 1 + 2 * ma, ma)
        for m in range(orders):
            cut = slice(q * width, (q + 1) * width)
            rows_all[place * orders + m, 0] = jnp.concatenate(
                [rows_ref[2 * m][:, cut], rows_ref[2 * m + 1][:, cut]], axis=1)
    pl.semaphore_wait(barrier, len(partners))

    def copy(src, dst, ssem, rsem, device):
        return pltpu.make_async_remote_copy(
            src_ref=src, dst_ref=dst, send_sem=ssem, recv_sem=rsem, device_id=device, device_id_type=MESH)

    row_copies = {}

    def send_rows(k, have, via):
        slot = have + via
        row_copies[k, slot] = copy(rows_all.at[k, have], rows_all.at[k, slot], row_ssem.at[k, slot], row_rsem.at[k, slot],
                                   peer(via))
        row_copies[k, slot].start()

    def first(k):
        for via in (FAR, NEAR, CORE):
            send_rows(k, 0, via)

    first(0)

    leg_copy.wait()
    total = leg_ref.shape[2]
    degree = lax.broadcasted_iota(jnp.int32, (orders, rows, total), 2)
    order = lax.broadcasted_iota(jnp.int32, (orders, rows, total), 0) + mine * orders
    table = jnp.where(degree >= order, leg_ref[...].astype(jnp.float32), 0.0)
    turned = table.reshape(orders * rows, total).T
    for at in range(GROUP):
        parts = []
        for b in range(blocks):
            start = (b * GROUP + at) * deg
            part_rows = turned[start:start + deg]
            if dq > deg:
                part_rows = jnp.concatenate([part_rows, jnp.zeros((dq - deg, orders * rows), jnp.float32)], axis=0)
            parts.append(part_rows)
        tab_send[at] = jnp.concatenate(parts, axis=0).astype(jnp.bfloat16)

    tab_copies = {}
    for slot in (FAR, NEAR, FAR + NEAR, FAR + CORE, NEAR + CORE, FAR + NEAR + CORE, CORE):
        tab_copies[slot] = copy(tab_send.at[member(slot)], tab_all.at[slot], tab_ssem.at[slot], tab_rsem.at[slot], peer(slot))
        tab_copies[slot].start()
    first(1)
    spec_copies = []
    for step in range(1, ma):
        to = other_ma(step)
        spec_copies.append(copy(spec_ref.at[to], spec_all.at[mine], spec_ssem.at[step], spec_rsem.at[step], (lat, to)))
        spec_copies[-1].start()
    spec_all[mine] = spec_ref[mine]

    def spread(k):
        row_copies[k, FAR].wait_recv()
        send_rows(k, FAR, NEAR)
        send_rows(k, FAR, CORE)
        if k + 2 < chunks:
            first(k + 2)
        row_copies[k, NEAR].wait_recv()
        send_rows(k, NEAR, CORE)

    def spread_last(k):
        row_copies[k, FAR + NEAR].wait_recv()
        send_rows(k, FAR + NEAR, CORE)

    part_copies = {}

    def multiply(k):
        m = k % orders
        if k == 0:
            for slot in tab_copies:
                tab_copies[slot].wait_recv()
            tabs = [tab_send[spot]] + [tab_all[slot] for slot in range(1, GROUP)]
            for order_at in range(orders):
                lhs[order_at] = jnp.concatenate(
                    [t.astype(jnp.float32)[:, order_at * rows:(order_at + 1) * rows] for t in tabs], axis=1
                ).astype(jnp.bfloat16)
        for slot in (CORE, NEAR + CORE, FAR + CORE, FAR + NEAR + CORE):
            row_copies[k, slot].wait_recv()
        product = jnp.dot(lhs[m], rows_all[k].reshape(GROUP * rows, 2 * width), preferred_element_type=jnp.float32)
        part[k] = product.reshape(blocks, dq, 2 * width)
        for step in range(1, blocks):
            to = other_block(step)
            part_copies[k, step] = copy(part.at[k, to], part_recv.at[k, step], part_ssem.at[k, step], part_rsem.at[k, step],
                                        (to * GROUP + spot, mine))
            part_copies[k, step].start()

    w_copies = []

    def finish(k):
        value = part[k, block]
        for step in range(1, blocks):
            part_copies[k, step].wait_recv()
            value = value + part_recv[k, step]
        step = (k // orders + 1) % ma
        m = k % orders
        q = other_ma(step)
        value_all[q * orders + m] = value
        if k == 0:
            for each in spec_copies:
                each.wait_recv()
        real_grad = value[:, :width]
        imag_grad = value[:, width:]
        stored = spec_all[q].astype(jnp.float32)
        real_store = stored[2 * m * dq:(2 * m + 1) * dq]
        imag_store = stored[(2 * m + 1) * dq:(2 * m + 2) * dq]
        real = real_store * real_grad + imag_store * imag_grad
        imag = real_store * imag_grad - imag_store * real_grad
        if m == 0:
            wpart[step, 0] = real
            wpart[step, 1] = imag
        else:
            wpart[step, 0] += real
            wpart[step, 1] += imag
        if m == orders - 1 and step > 0:
            w_copies.append(copy(wpart.at[step], wrecv.at[step], w_ssem.at[step], w_rsem.at[step], (lat, q)))
            w_copies[-1].start()

    spread(0)
    spread_last(0)
    for k in range(chunks):
        if k + 1 < chunks:
            spread(k + 1)
        multiply(k)
        if k + 1 < chunks:
            spread_last(k + 1)
    for k in range(chunks):
        finish(k)

    for m in range(orders):
        for r in range(2):
            grads_ref[m, r] = jnp.concatenate(
                [value_all[q * orders + m][:, r * width:(r + 1) * width] for q in range(ma)], axis=1)
    weight = wpart[0]
    for step in range(1, ma):
        w_copies[step - 1].wait_recv()
        weight = weight + wrecv[step]
    wgrad_ref[...] = weight

    for each in [*tab_copies.values(), *row_copies.values(), *part_copies.values(), *spec_copies, *w_copies]:
        each.wait_send()


def body(n, ma, grad_fourier, legendre, spectra, filter_weight):
    orders, rows, _, chans = grad_fourier.shape
    deg = filter_weight.shape[0]
    dq = -(-deg // 8) * 8
    width = chans // ma
    chunks = ma * orders
    blocks = n // GROUP
    flat_rows = grad_fourier.transpose(0, 2, 1, 3).reshape(2 * orders, rows, chans)
    spec = jnp.pad(spectra, ((0, dq - deg), (0, 0), (0, 0), (0, 0))).transpose(1, 2, 0, 3)
    spec = spec.reshape(ma, 2 * orders * dq, width)
    vmem = pl.BlockSpec(memory_space=pltpu.VMEM)
    dma = pltpu.SemaphoreType.DMA
    grads, wgrad = pl.pallas_call(
        functools.partial(kernel, (n, ma, orders, rows, deg, dq, chans)),
        out_shape=(
            jax.ShapeDtypeStruct((orders, 2, dq, chans), jnp.float32),
            jax.ShapeDtypeStruct((2, dq, width), jnp.float32),
        ),
        in_specs=[pl.BlockSpec(memory_space=pltpu.HBM), vmem, vmem],
        out_specs=(vmem, vmem),
        scratch_shapes=[
            pltpu.VMEM(legendre.shape, jnp.bfloat16),
            pltpu.VMEM((GROUP, blocks * dq, orders * rows), jnp.bfloat16),
            pltpu.VMEM((GROUP, blocks * dq, orders * rows), jnp.bfloat16),
            pltpu.VMEM((orders, blocks * dq, GROUP * rows), jnp.bfloat16),
            pltpu.VMEM((chunks, GROUP, rows, 2 * width), jnp.bfloat16),
            pltpu.VMEM((chunks, blocks, dq, 2 * width), jnp.float32),
            pltpu.VMEM((chunks, blocks, dq, 2 * width), jnp.float32),
            pltpu.VMEM((chunks, dq, 2 * width), jnp.float32),
            pltpu.VMEM((ma, 2 * orders * dq, width), jnp.bfloat16),
            pltpu.VMEM((ma, 2, dq, width), jnp.float32),
            pltpu.VMEM((ma, 2, dq, width), jnp.float32),
            dma(()),
            dma((GROUP,)), dma((GROUP,)),
            dma((chunks, GROUP)), dma((chunks, GROUP)),
            dma((chunks, blocks)), dma((chunks, blocks)),
            dma((ma,)), dma((ma,)),
            dma((ma,)), dma((ma,)),
        ],
        compiler_params=pltpu.CompilerParams(
            collective_id=0, has_side_effects=True, vmem_limit_bytes=24 * 1024 * 1024),
        cost_estimate=pl.CostEstimate(
            flops=4 * orders * blocks * dq * GROUP * rows * chans, bytes_accessed=8 * orders * dq * chans, transcendentals=0),
    )(legendre, flat_rows, spec)
    grads = grads[:, :, :deg].transpose(2, 0, 1, 3)
    real_grad = grads[:, :, 0, :]
    imag_grad = grads[:, :, 1, :]
    real_weight = filter_weight[:, None, 0, :]
    imag_weight = filter_weight[:, None, 1, :]
    input_grad = jnp.stack(
        [
            real_weight * real_grad + imag_weight * imag_grad,
            real_weight * imag_grad - imag_weight * real_grad,
        ],
        axis=2,
    )
    return input_grad, wgrad[:, :deg].transpose(1, 0, 2)


def solution(mesh):
    in_specs = (
        P("ma", "lat", None, None),
        P("ma", "lat", None),
        P("lat", None, None, "ma"),
        P("lat", None, None),
    )
    out_specs = (P("lat", "ma", None, None), P("lat", None, "ma"))
    fn = functools.partial(body, mesh.shape["lat"], mesh.shape["ma"])
    return jax.shard_map(fn, mesh=mesh, in_specs=in_specs, out_specs=out_specs, check_vma=False)
```

```python
import functools

import jax
import jax.numpy as jnp
from jax import lax
from jax.experimental import pallas as pl
from jax.experimental.pallas import tpu as pltpu
from jax.sharding import PartitionSpec as P

MESH = pl.DeviceIdType.MESH
GROUP = 8
CORE, NEAR, FAR = 1, 2, 4


def kernel(sizes, leg_hbm, rows_ref, spec_ref, grads_ref, wgrad_ref, leg_ref, tab_send, tab_all, lhs, rows_out, rows_all,
           part, part_recv, value_all, spec_all, wpart, wrecv, leg_sem, tab_ssem, tab_rsem, row_ssem, row_rsem, part_ssem,
           part_rsem, spec_ssem, spec_rsem, w_ssem, w_rsem):
    n, ma, orders, rows, deg, dq, chans, cuts = sizes
    blocks = n // GROUP
    chunks = ma * cuts
    width = chans // ma
    lanes = 2 * width // cuts
    lat = lax.axis_index("lat")
    mine = lax.axis_index("ma")
    spot = lax.rem(lat, GROUP)
    block = lax.div(lat, GROUP)
    bits = [lax.rem(lax.div(spot, 1 << b), 2) for b in range(3)]
    own = [bits[0], 1 - bits[0]]

    def member(slot):
        at = 0
        for b in range(3):
            bit = 1 - bits[b] if slot >> b & 1 else bits[b]
            at = at + bit * (1 << b)
        return at

    def peer(slot, step=0):
        return (other_block(step) * GROUP + member(slot), mine)

    def other_block(step):
        return lax.rem(block + step, blocks)

    def other_ma(step):
        return lax.rem(mine + step, ma)

    barrier = pltpu.get_barrier_semaphore()
    partners = [peer(slot) for slot in range(1, GROUP)]
    partners += [peer(slot, step) for step in range(1, blocks) for slot in (0, CORE)]
    partners += [(lat, other_ma(step)) for step in range(1, ma)]
    for device in partners:
        pl.semaphore_signal(barrier, inc=1, device_id=device, device_id_type=MESH)
    leg_copy = pltpu.make_async_copy(leg_hbm, leg_ref, leg_sem)
    leg_copy.start()

    for q in range(ma):
        place = lax.rem(q - mine - 1 + 2 * ma, ma)
        cut = slice(q * width, (q + 1) * width)
        for e in range(2):
            both = jnp.concatenate([rows_ref[2 * own[e]][:, cut], rows_ref[2 * own[e] + 1][:, cut]], axis=1)
            for part_at in range(cuts):
                piece = both[:, part_at * lanes:(part_at + 1) * lanes]
                if e == 0:
                    rows_all[place * cuts + part_at, 0] = piece
                else:
                    rows_out[place * cuts + part_at] = piece
    pl.semaphore_wait(barrier, len(partners))

    def copy(src, dst, ssem, rsem, device):
        return pltpu.make_async_remote_copy(
            src_ref=src, dst_ref=dst, send_sem=ssem, recv_sem=rsem, device_id=device, device_id_type=MESH)

    row_copies = {}

    def send_rows(k, src, slot, via):
        row_copies[k, slot] = copy(src, rows_all.at[k, slot], row_ssem.at[k, slot], row_rsem.at[k, slot], peer(via))
        row_copies[k, slot].start()

    def first(k):
        for via in (FAR, FAR + CORE, NEAR, NEAR + CORE, CORE):
            send_rows(k, rows_out.at[k] if via & CORE else rows_all.at[k, 0], via, via)

    first(0)

    leg_copy.wait()
    total = leg_ref.shape[2]
    degree = lax.broadcasted_iota(jnp.int32, (orders, rows, total), 2)
    order = lax.broadcasted_iota(jnp.int32, (orders, rows, total), 0) + mine * orders
    table = jnp.where(degree >= order, leg_ref[...].astype(jnp.float32), 0.0)
    turned = table.reshape(orders * rows, total).T
    half = blocks // 2
    for pair in range(GROUP // 2):
        halves = []
        for f in range(2):
            parts = []
            for b in range(f * half, (f + 1) * half):
                for c in range(2):
                    start = (b * GROUP + pair * 2 + c) * deg
                    parts.append(turned[start:start + deg])
                    if dq > deg:
                        parts.append(jnp.zeros((dq - deg, orders * rows), jnp.float32))
            halves.append(jnp.concatenate(parts, axis=0))
        for m in range(orders):
            tab_send[pair * 2 + m] = jnp.concatenate(
                [each[:, m * rows:(m + 1) * rows] for each in halves], axis=1).astype(jnp.bfloat16)

    tab_copies = {}
    for slot in (FAR, NEAR, FAR + NEAR, FAR + CORE, NEAR + CORE, FAR + NEAR + CORE, CORE):
        tab_copies[slot] = copy(tab_send.at[member(slot)], tab_all.at[slot], tab_ssem.at[slot], tab_rsem.at[slot], peer(slot))
        tab_copies[slot].start()
    first(1)
    spec_copies = []
    for step in range(1, ma):
        to = other_ma(step)
        spec_copies.append(copy(spec_ref.at[to], spec_all.at[mine], spec_ssem.at[step], spec_rsem.at[step], (lat, to)))
        spec_copies[-1].start()
    spec_all[mine] = spec_ref[mine]

    def spread(k):
        for slot in (FAR, FAR + CORE):
            row_copies[k, slot].wait_recv()
            send_rows(k, rows_all.at[k, slot], slot + NEAR, NEAR)
        if k + 2 < chunks:
            first(k + 2)

    part_copies = {}

    def multiply(k):
        if k == 0:
            for slot in tab_copies:
                tab_copies[slot].wait_recv()
            tabs = [tab_send[spot]] + [tab_all[slot] for slot in range(1, GROUP)]
            tabs = [t.astype(jnp.float32) for t in tabs]
            lhs[...] = jnp.concatenate(
                [jnp.concatenate([t[:, f * rows:(f + 1) * rows] for t in tabs], axis=1) for f in range(2)], axis=0
            ).astype(jnp.bfloat16)
        for slot in (CORE, NEAR, NEAR + CORE, FAR + NEAR, FAR + NEAR + CORE):
            row_copies[k, slot].wait_recv()
        product = jnp.dot(lhs[...], rows_all[k].reshape(GROUP * rows, lanes), preferred_element_type=jnp.float32)
        part[k] = product.reshape(2 * blocks, dq, lanes)
        for step in range(1, blocks + 1):
            step = step % blocks
            for e in range(2):
                if step or e:
                    part_copies[k, step, e] = copy(
                        part.at[k, other_block(step) * 2 + own[e]], part_recv.at[k, step, e], part_ssem.at[k, step, e],
                        part_rsem.at[k, step, e], peer(e * CORE, step))
                    part_copies[k, step, e].start()

    w_copies = []

    def finish(turn):
        step = (turn + 1) % ma
        q = other_ma(step)
        if turn == 0:
            for each in spec_copies:
                each.wait_recv()
        real, imag = 0.0, 0.0
        for e in range(2):
            pieces = []
            for k in range(turn * cuts, (turn + 1) * cuts):
                piece = part[k, block * 2 + own[0]] if e == 0 else None
                for s in range(0 if e else 1, blocks):
                    part_copies[k, s, e].wait_recv()
                    piece = part_recv[k, s, e] if piece is None else piece + part_recv[k, s, e]
                pieces.append(piece)
            value = jnp.concatenate(pieces, axis=1)
            value_all[q * orders + own[e]] = value
            real_grad = value[:, :width]
            imag_grad = value[:, width:]
            stored = spec_all[q, own[e]].astype(jnp.float32)
            real_store = stored[:dq]
            imag_store = stored[dq:]
            real = real + real_store * real_grad + imag_store * imag_grad
            imag = imag + real_store * imag_grad - imag_store * real_grad
        wpart[step, 0] = real
        wpart[step, 1] = imag
        if step > 0:
            w_copies.append(copy(wpart.at[step], wrecv.at[step], w_ssem.at[step], w_rsem.at[step], (lat, q)))
            w_copies[-1].start()

    spread(0)
    for k in range(chunks):
        if k + 1 < chunks:
            spread(k + 1)
        multiply(k)
    for turn in range(ma):
        finish(turn)

    for m in range(orders):
        for r in range(2):
            grads_ref[m, r] = jnp.concatenate(
                [value_all[q * orders + m][:, r * width:(r + 1) * width] for q in range(ma)], axis=1)
    weight = wpart[0]
    for step in range(1, ma):
        w_copies[step - 1].wait_recv()
        weight = weight + wrecv[step]
    wgrad_ref[...] = weight

    for each in [*tab_copies.values(), *row_copies.values(), *part_copies.values(), *spec_copies, *w_copies]:
        each.wait_send()


def body(n, ma, grad_fourier, legendre, spectra, filter_weight):
    orders, rows, _, chans = grad_fourier.shape
    deg = filter_weight.shape[0]
    dq = -(-deg // 8) * 8
    width = chans // ma
    cuts = max(2 * width // 128, 1)
    chunks = ma * cuts
    lanes = 2 * width // cuts
    blocks = n // GROUP
    flat_rows = grad_fourier.transpose(0, 2, 1, 3).reshape(2 * orders, rows, chans)
    spec = jnp.pad(spectra, ((0, dq - deg), (0, 0), (0, 0), (0, 0))).transpose(1, 2, 0, 3)
    spec = spec.reshape(ma, orders, 2 * dq, width)
    vmem = pl.BlockSpec(memory_space=pltpu.VMEM)
    dma = pltpu.SemaphoreType.DMA
    grads, wgrad = pl.pallas_call(
        functools.partial(kernel, (n, ma, orders, rows, deg, dq, chans, cuts)),
        out_shape=(
            jax.ShapeDtypeStruct((orders, 2, dq, chans), jnp.float32),
            jax.ShapeDtypeStruct((2, dq, width), jnp.float32),
        ),
        in_specs=[pl.BlockSpec(memory_space=pltpu.HBM), vmem, vmem],
        out_specs=(vmem, vmem),
        scratch_shapes=[
            pltpu.VMEM(legendre.shape, jnp.bfloat16),
            pltpu.VMEM((GROUP, blocks * dq, 2 * rows), jnp.bfloat16),
            pltpu.VMEM((GROUP, blocks * dq, 2 * rows), jnp.bfloat16),
            pltpu.VMEM((2 * blocks * dq, GROUP * rows), jnp.bfloat16),
            pltpu.VMEM((chunks, rows, lanes), jnp.bfloat16),
            pltpu.VMEM((chunks, GROUP, rows, lanes), jnp.bfloat16),
            pltpu.VMEM((chunks, 2 * blocks, dq, lanes), jnp.float32),
            pltpu.VMEM((chunks, blocks, 2, dq, lanes), jnp.float32),
            pltpu.VMEM((ma * orders, dq, 2 * width), jnp.float32),
            pltpu.VMEM((ma, orders, 2 * dq, width), jnp.bfloat16),
            pltpu.VMEM((ma, 2, dq, width), jnp.float32),
            pltpu.VMEM((ma, 2, dq, width), jnp.float32),
            dma(()),
            dma((GROUP,)), dma((GROUP,)),
            dma((chunks, GROUP)), dma((chunks, GROUP)),
            dma((chunks, blocks, 2)), dma((chunks, blocks, 2)),
            dma((ma,)), dma((ma,)),
            dma((ma,)), dma((ma,)),
        ],
        compiler_params=pltpu.CompilerParams(
            collective_id=0, has_side_effects=True, vmem_limit_bytes=24 * 1024 * 1024),
        cost_estimate=pl.CostEstimate(
            flops=4 * orders * blocks * dq * GROUP * rows * chans, bytes_accessed=8 * orders * dq * chans, transcendentals=0),
    )(legendre, flat_rows, spec)
    grads = grads[:, :, :deg].transpose(2, 0, 1, 3)
    real_grad = grads[:, :, 0, :]
    imag_grad = grads[:, :, 1, :]
    real_weight = filter_weight[:, None, 0, :]
    imag_weight = filter_weight[:, None, 1, :]
    input_grad = jnp.stack(
        [
            real_weight * real_grad + imag_weight * imag_grad,
            real_weight * imag_grad - imag_weight * real_grad,
        ],
        axis=2,
    )
    return input_grad, wgrad[:, :deg].transpose(1, 0, 2)


def solution(mesh):
    in_specs = (
        P("ma", "lat", None, None),
        P("ma", "lat", None),
        P("lat", None, None, "ma"),
        P("lat", None, None),
    )
    out_specs = (P("lat", "ma", None, None), P("lat", None, "ma"))
    fn = functools.partial(body, mesh.shape["lat"], mesh.shape["ma"])
    return jax.shard_map(fn, mesh=mesh, in_specs=in_specs, out_specs=out_specs, check_vma=False)
```

```python
import functools

import jax
import jax.numpy as jnp
from jax import lax
from jax.experimental import pallas as pl
from jax.experimental.pallas import tpu as pltpu
from jax.sharding import PartitionSpec as P

MESH = pl.DeviceIdType.MESH
GROUP = 8
CORE, NEAR, FAR = 1, 2, 4


def kernel(sizes, leg_ref, rows_ref, spec_ref, grads_ref, wgrad_ref, tab_send, tab_all, lhs, rows_out, rows_all,
           part, part_recv, value_all, spec_all, wpart, wrecv, tab_ssem, tab_rsem, row_ssem, row_rsem, part_ssem,
           part_rsem, spec_ssem, spec_rsem, w_ssem, w_rsem):
    n, ma, orders, rows, deg, dq, chans, cuts = sizes
    blocks = n // GROUP
    chunks = ma * cuts
    width = chans // ma
    lanes = 2 * width // cuts
    lat = lax.axis_index("lat")
    mine = lax.axis_index("ma")
    spot = lax.rem(lat, GROUP)
    block = lax.div(lat, GROUP)
    bits = [lax.rem(lax.div(spot, 1 << b), 2) for b in range(3)]
    own = [bits[0], 1 - bits[0]]

    def member(slot):
        at = 0
        for b in range(3):
            bit = 1 - bits[b] if slot >> b & 1 else bits[b]
            at = at + bit * (1 << b)
        return at

    def peer(slot, step=0):
        return (other_block(step) * GROUP + member(slot), mine)

    def other_block(step):
        return lax.rem(block + step, blocks)

    def other_ma(step):
        return lax.rem(mine + step, ma)

    barrier = pltpu.get_barrier_semaphore()
    partners = [peer(slot) for slot in range(1, GROUP)]
    partners += [peer(slot, step) for step in range(1, blocks) for slot in (0, CORE)]
    partners += [(lat, other_ma(step)) for step in range(1, ma)]
    for device in partners:
        pl.semaphore_signal(barrier, inc=1, device_id=device, device_id_type=MESH)

    for q in range(ma):
        place = lax.rem(q - mine - 1 + 2 * ma, ma)
        cut = slice(q * width, (q + 1) * width)
        for e in range(2):
            both = jnp.concatenate([rows_ref[2 * own[e]][:, cut], rows_ref[2 * own[e] + 1][:, cut]], axis=1)
            for part_at in range(cuts):
                piece = both[:, part_at * lanes:(part_at + 1) * lanes]
                if e == 0:
                    rows_all[place * cuts + part_at, 0] = piece
                else:
                    rows_out[place * cuts + part_at] = piece
    pl.semaphore_wait(barrier, len(partners))

    def copy(src, dst, ssem, rsem, device):
        return pltpu.make_async_remote_copy(
            src_ref=src, dst_ref=dst, send_sem=ssem, recv_sem=rsem, device_id=device, device_id_type=MESH)

    row_copies = {}

    def send_rows(k, src, slot, via):
        row_copies[k, slot] = copy(src, rows_all.at[k, slot], row_ssem.at[k, slot], row_rsem.at[k, slot], peer(via))
        row_copies[k, slot].start()

    def first(k):
        for via in (FAR, FAR + CORE, NEAR, NEAR + CORE, CORE):
            send_rows(k, rows_out.at[k] if via & CORE else rows_all.at[k, 0], via, via)

    first(0)

    turned = leg_ref[...].astype(jnp.float32).reshape(orders * rows, leg_ref.shape[2]).T
    half = blocks // 2
    for pair in range(GROUP // 2):
        halves = []
        for f in range(2):
            parts = []
            for b in range(f * half, (f + 1) * half):
                for c in range(2):
                    start = (b * GROUP + pair * 2 + c) * deg
                    parts.append(turned[start:start + deg])
                    if dq > deg:
                        parts.append(jnp.zeros((dq - deg, orders * rows), jnp.float32))
            halves.append(jnp.concatenate(parts, axis=0))
        for m in range(orders):
            tab_send[pair * 2 + m] = jnp.concatenate(
                [each[:, m * rows:(m + 1) * rows] for each in halves], axis=1).astype(jnp.bfloat16)

    tab_copies = {}
    for slot in (FAR, NEAR, FAR + NEAR, FAR + CORE, NEAR + CORE, FAR + NEAR + CORE, CORE):
        tab_copies[slot] = copy(tab_send.at[member(slot)], tab_all.at[slot], tab_ssem.at[slot], tab_rsem.at[slot], peer(slot))
        tab_copies[slot].start()
    first(1)
    spec_copies = []
    for step in range(1, ma):
        to = other_ma(step)
        spec_copies.append(copy(spec_ref.at[to], spec_all.at[mine], spec_ssem.at[step], spec_rsem.at[step], (lat, to)))
        spec_copies[-1].start()
    spec_all[mine] = spec_ref[mine]

    def spread(k):
        for slot in (FAR, FAR + CORE):
            row_copies[k, slot].wait_recv()
            send_rows(k, rows_all.at[k, slot], slot + NEAR, NEAR)
        if k + 2 < chunks:
            first(k + 2)

    part_copies = {}

    def multiply(k):
        if k == 0:
            for slot in tab_copies:
                tab_copies[slot].wait_recv()
            tabs = [tab_send[spot]] + [tab_all[slot] for slot in range(1, GROUP)]
            tabs = [t.astype(jnp.float32) for t in tabs]
            lhs[...] = jnp.concatenate(
                [jnp.concatenate([t[:, f * rows:(f + 1) * rows] for t in tabs], axis=1) for f in range(2)], axis=0
            ).astype(jnp.bfloat16)
        for slot in (CORE, NEAR, NEAR + CORE, FAR + NEAR, FAR + NEAR + CORE):
            row_copies[k, slot].wait_recv()
        product = jnp.dot(lhs[...], rows_all[k].reshape(GROUP * rows, lanes), preferred_element_type=jnp.float32)
        part[k] = product.reshape(2 * blocks, dq, lanes)
        for step in range(1, blocks + 1):
            step = step % blocks
            for e in range(2):
                if step or e:
                    part_copies[k, step, e] = copy(
                        part.at[k, other_block(step) * 2 + own[e]], part_recv.at[k, step, e], part_ssem.at[k, step, e],
                        part_rsem.at[k, step, e], peer(e * CORE, step))
                    part_copies[k, step, e].start()

    w_copies = []

    def finish(turn):
        step = (turn + 1) % ma
        q = other_ma(step)
        if turn == 0:
            for each in spec_copies:
                each.wait_recv()
        real, imag = 0.0, 0.0
        for e in range(2):
            pieces = []
            for k in range(turn * cuts, (turn + 1) * cuts):
                piece = part[k, block * 2 + own[0]] if e == 0 else None
                for s in range(0 if e else 1, blocks):
                    part_copies[k, s, e].wait_recv()
                    piece = part_recv[k, s, e] if piece is None else piece + part_recv[k, s, e]
                pieces.append(piece)
            value = jnp.concatenate(pieces, axis=1)
            value_all[q * orders + own[e]] = value
            real_grad = value[:, :width]
            imag_grad = value[:, width:]
            stored = spec_all[q, own[e]].astype(jnp.float32)
            real_store = stored[:dq]
            imag_store = stored[dq:]
            real = real + real_store * real_grad + imag_store * imag_grad
            imag = imag + real_store * imag_grad - imag_store * real_grad
        wpart[step, 0] = real
        wpart[step, 1] = imag
        if step > 0:
            w_copies.append(copy(wpart.at[step], wrecv.at[step], w_ssem.at[step], w_rsem.at[step], (lat, q)))
            w_copies[-1].start()

    spread(0)
    for k in range(chunks):
        if k + 1 < chunks:
            spread(k + 1)
        multiply(k)
        if k % cuts == max(cuts - 2, 0) and k >= cuts:
            finish(k // cuts - 1)
    finish(ma - 1)

    for m in range(orders):
        for r in range(2):
            grads_ref[m, r] = jnp.concatenate(
                [value_all[q * orders + m][:, r * width:(r + 1) * width] for q in range(ma)], axis=1)
    weight = wpart[0]
    for step in range(1, ma):
        w_copies[step - 1].wait_recv()
        weight = weight + wrecv[step]
    wgrad_ref[...] = weight

    for each in [*tab_copies.values(), *row_copies.values(), *part_copies.values(), *spec_copies, *w_copies]:
        each.wait_send()


def body(n, ma, grad_fourier, legendre, spectra, filter_weight):
    orders, rows, _, chans = grad_fourier.shape
    deg = filter_weight.shape[0]
    dq = -(-deg // 8) * 8
    width = chans // ma
    cuts = max(2 * width // 128, 1)
    chunks = ma * cuts
    lanes = 2 * width // cuts
    blocks = n // GROUP
    flat_rows = grad_fourier.transpose(0, 2, 1, 3).reshape(2 * orders, rows, chans)
    degree = lax.broadcasted_iota(jnp.int32, legendre.shape, 2)
    order = lax.broadcasted_iota(jnp.int32, legendre.shape, 0) + lax.axis_index("ma") * orders
    table = jnp.where(degree >= order, legendre, jnp.zeros_like(legendre))
    spec = jnp.pad(spectra, ((0, dq - deg), (0, 0), (0, 0), (0, 0))).transpose(1, 2, 0, 3)
    spec = spec.reshape(ma, orders, 2 * dq, width)
    vmem = pl.BlockSpec(memory_space=pltpu.VMEM)
    dma = pltpu.SemaphoreType.DMA
    grads, wgrad = pl.pallas_call(
        functools.partial(kernel, (n, ma, orders, rows, deg, dq, chans, cuts)),
        out_shape=(
            jax.ShapeDtypeStruct((orders, 2, dq, chans), jnp.float32),
            jax.ShapeDtypeStruct((2, dq, width), jnp.float32),
        ),
        in_specs=[vmem] * 3,
        out_specs=(vmem, vmem),
        scratch_shapes=[
            pltpu.VMEM((GROUP, blocks * dq, 2 * rows), jnp.bfloat16),
            pltpu.VMEM((GROUP, blocks * dq, 2 * rows), jnp.bfloat16),
            pltpu.VMEM((2 * blocks * dq, GROUP * rows), jnp.bfloat16),
            pltpu.VMEM((chunks, rows, lanes), jnp.bfloat16),
            pltpu.VMEM((chunks, GROUP, rows, lanes), jnp.bfloat16),
            pltpu.VMEM((chunks, 2 * blocks, dq, lanes), jnp.float32),
            pltpu.VMEM((chunks, blocks, 2, dq, lanes), jnp.float32),
            pltpu.VMEM((ma * orders, dq, 2 * width), jnp.float32),
            pltpu.VMEM((ma, orders, 2 * dq, width), jnp.bfloat16),
            pltpu.VMEM((ma, 2, dq, width), jnp.float32),
            pltpu.VMEM((ma, 2, dq, width), jnp.float32),
            dma((GROUP,)), dma((GROUP,)),
            dma((chunks, GROUP)), dma((chunks, GROUP)),
            dma((chunks, blocks, 2)), dma((chunks, blocks, 2)),
            dma((ma,)), dma((ma,)),
            dma((ma,)), dma((ma,)),
        ],
        compiler_params=pltpu.CompilerParams(
            collective_id=0, has_side_effects=True, vmem_limit_bytes=24 * 1024 * 1024),
        cost_estimate=pl.CostEstimate(
            flops=4 * orders * blocks * dq * GROUP * rows * chans, bytes_accessed=8 * orders * dq * chans, transcendentals=0),
    )(table, flat_rows, spec)
    grads = grads[:, :, :deg].transpose(2, 0, 1, 3)
    real_grad = grads[:, :, 0, :]
    imag_grad = grads[:, :, 1, :]
    real_weight = filter_weight[:, None, 0, :]
    imag_weight = filter_weight[:, None, 1, :]
    input_grad = jnp.stack(
        [
            real_weight * real_grad + imag_weight * imag_grad,
            real_weight * imag_grad - imag_weight * real_grad,
        ],
        axis=2,
    )
    return input_grad, wgrad[:, :deg].transpose(1, 0, 2)


def solution(mesh):
    in_specs = (
        P("ma", "lat", None, None),
        P("ma", "lat", None),
        P("lat", None, None, "ma"),
        P("lat", None, None),
    )
    out_specs = (P("lat", "ma", None, None), P("lat", None, "ma"))
    fn = functools.partial(body, mesh.shape["lat"], mesh.shape["ma"])
    return jax.shard_map(fn, mesh=mesh, in_specs=in_specs, out_specs=out_specs, check_vma=False)
```

```python
import functools

import jax
import jax.numpy as jnp
from jax import lax
from jax.experimental import pallas as pl
from jax.experimental.pallas import tpu as pltpu
from jax.sharding import PartitionSpec as P

MESH = pl.DeviceIdType.MESH
GROUP = 8
CORE, NEAR, FAR = 1, 2, 4


def kernel(sizes, leg_hbm, rows_ref, spec_ref, grads_ref, wgrad_ref, leg_ref, tab_send, tab_all, lhs, rows_out, rows_all,
           part, part_recv, value_all, spec_all, wpart, wrecv, leg_sem, tab_ssem, tab_rsem, row_ssem, row_rsem, part_ssem,
           part_rsem, spec_ssem, spec_rsem, w_ssem, w_rsem):
    n, ma, orders, rows, deg, dq, chans, cuts = sizes
    blocks = n // GROUP
    chunks = ma * cuts
    width = chans // ma
    lanes = 2 * width // cuts
    ahead = min(3, chunks)
    lat = lax.axis_index("lat")
    mine = lax.axis_index("ma")
    spot = lax.rem(lat, GROUP)
    block = lax.div(lat, GROUP)
    bits = [lax.rem(lax.div(spot, 1 << b), 2) for b in range(3)]
    own = [bits[0], 1 - bits[0]]

    def member(slot):
        at = 0
        for b in range(3):
            bit = 1 - bits[b] if slot >> b & 1 else bits[b]
            at = at + bit * (1 << b)
        return at

    def peer(slot, step=0):
        return (other_block(step) * GROUP + member(slot), mine)

    def other_block(step):
        return lax.rem(block + step, blocks)

    def other_ma(step):
        return lax.rem(mine + step, ma)

    barrier = pltpu.get_barrier_semaphore()
    partners = [peer(slot) for slot in range(1, GROUP)]
    partners += [peer(slot, step) for step in range(1, blocks) for slot in (0, CORE)]
    partners += [(lat, other_ma(step)) for step in range(1, ma)]
    for device in partners:
        pl.semaphore_signal(barrier, inc=1, device_id=device, device_id_type=MESH)
    leg_copy = pltpu.make_async_copy(leg_hbm, leg_ref, leg_sem)
    leg_copy.start()

    for q in range(ma):
        place = lax.rem(q - mine - 1 + 2 * ma, ma)
        cut = slice(q * width, (q + 1) * width)
        for e in range(2):
            both = jnp.concatenate([rows_ref[2 * own[e]][:, cut], rows_ref[2 * own[e] + 1][:, cut]], axis=1)
            for part_at in range(cuts):
                piece = both[:, part_at * lanes:(part_at + 1) * lanes]
                if e == 0:
                    rows_all[place * cuts + part_at, 0] = piece
                else:
                    rows_out[place * cuts + part_at] = piece
    pl.semaphore_wait(barrier, len(partners))

    def copy(src, dst, ssem, rsem, device):
        return pltpu.make_async_remote_copy(
            src_ref=src, dst_ref=dst, send_sem=ssem, recv_sem=rsem, device_id=device, device_id_type=MESH)

    row_copies = {}

    def send_rows(k, src, slot, via):
        row_copies[k, slot] = copy(src, rows_all.at[k, slot], row_ssem.at[k, slot], row_rsem.at[k, slot], peer(via))
        row_copies[k, slot].start()

    def first(k):
        for via in (FAR, FAR + CORE, NEAR, NEAR + CORE, CORE):
            send_rows(k, rows_out.at[k] if via & CORE else rows_all.at[k, 0], via, via)

    first(0)

    leg_copy.wait()
    total = leg_ref.shape[2]
    degree = lax.broadcasted_iota(jnp.int32, (orders, rows, total), 2)
    order = lax.broadcasted_iota(jnp.int32, (orders, rows, total), 0) + mine * orders
    table = jnp.where(degree >= order, leg_ref[...].astype(jnp.float32), 0.0)
    turned = table.reshape(orders * rows, total).T
    half = blocks // 2
    for pair in range(GROUP // 2):
        halves = []
        for f in range(2):
            parts = []
            for b in range(f * half, (f + 1) * half):
                for c in range(2):
                    start = (b * GROUP + pair * 2 + c) * deg
                    parts.append(turned[start:start + deg])
                    if dq > deg:
                        parts.append(jnp.zeros((dq - deg, orders * rows), jnp.float32))
            halves.append(jnp.concatenate(parts, axis=0))
        for m in range(orders):
            tab_send[pair * 2 + m] = jnp.concatenate(
                [each[:, m * rows:(m + 1) * rows] for each in halves], axis=1).astype(jnp.bfloat16)

    tab_copies = {}
    for slot in (FAR, NEAR, FAR + NEAR, FAR + CORE, NEAR + CORE, FAR + NEAR + CORE, CORE):
        tab_copies[slot] = copy(tab_send.at[member(slot)], tab_all.at[slot], tab_ssem.at[slot], tab_rsem.at[slot], peer(slot))
        tab_copies[slot].start()
    for k in range(1, ahead):
        first(k)
    spec_copies = []
    for step in range(1, ma):
        to = other_ma(step)
        spec_copies.append(copy(spec_ref.at[to], spec_all.at[mine], spec_ssem.at[step], spec_rsem.at[step], (lat, to)))
        spec_copies[-1].start()
    spec_all[mine] = spec_ref[mine]

    def spread(k):
        for slot in (FAR, FAR + CORE):
            row_copies[k, slot].wait_recv()
            send_rows(k, rows_all.at[k, slot], slot + NEAR, NEAR)
        if k + ahead < chunks:
            first(k + ahead)

    part_copies = {}

    def multiply(k):
        if k == 0:
            for slot in tab_copies:
                tab_copies[slot].wait_recv()
            tabs = [tab_send[spot]] + [tab_all[slot] for slot in range(1, GROUP)]
            tabs = [t.astype(jnp.float32) for t in tabs]
            lhs[...] = jnp.concatenate(
                [jnp.concatenate([t[:, f * rows:(f + 1) * rows] for t in tabs], axis=1) for f in range(2)], axis=0
            ).astype(jnp.bfloat16)
        for slot in (CORE, NEAR, NEAR + CORE, FAR + NEAR, FAR + NEAR + CORE):
            row_copies[k, slot].wait_recv()
        product = jnp.dot(lhs[...], rows_all[k].reshape(GROUP * rows, lanes), preferred_element_type=jnp.float32)
        part[k] = product.reshape(2 * blocks, dq, lanes)
        for step in range(1, blocks + 1):
            step = step % blocks
            for e in range(2):
                if step or e:
                    part_copies[k, step, e] = copy(
                        part.at[k, other_block(step) * 2 + own[e]], part_recv.at[k, step, e], part_ssem.at[k, step, e],
                        part_rsem.at[k, step, e], peer(e * CORE, step))
                    part_copies[k, step, e].start()

    w_copies = []

    def finish(turn):
        step = (turn + 1) % ma
        q = other_ma(step)
        if turn == 0:
            for each in spec_copies:
                each.wait_recv()
        real, imag = 0.0, 0.0
        for e in range(2):
            pieces = []
            for k in range(turn * cuts, (turn + 1) * cuts):
                piece = part[k, block * 2 + own[0]] if e == 0 else None
                for s in range(0 if e else 1, blocks):
                    part_copies[k, s, e].wait_recv()
                    piece = part_recv[k, s, e] if piece is None else piece + part_recv[k, s, e]
                pieces.append(piece)
            value = jnp.concatenate(pieces, axis=1)
            value_all[q * orders + own[e]] = value
            real_grad = value[:, :width]
            imag_grad = value[:, width:]
            stored = spec_all[q, own[e]].astype(jnp.float32)
            real_store = stored[:dq]
            imag_store = stored[dq:]
            real = real + real_store * real_grad + imag_store * imag_grad
            imag = imag + real_store * imag_grad - imag_store * real_grad
        wpart[step, 0] = real
        wpart[step, 1] = imag
        if step > 0:
            w_copies.append(copy(wpart.at[step], wrecv.at[step], w_ssem.at[step], w_rsem.at[step], (lat, q)))
            w_copies[-1].start()

    spread(0)
    for k in range(chunks):
        if k + 1 < chunks:
            spread(k + 1)
        multiply(k)
        if k % cuts == max(cuts - 2, 0) and k >= cuts:
            finish(k // cuts - 1)
    finish(ma - 1)

    for m in range(orders):
        for r in range(2):
            grads_ref[m, r] = jnp.concatenate(
                [value_all[q * orders + m][:, r * width:(r + 1) * width] for q in range(ma)], axis=1)
    weight = wpart[0]
    for step in range(1, ma):
        w_copies[step - 1].wait_recv()
        weight = weight + wrecv[step]
    wgrad_ref[...] = weight

    for each in [*tab_copies.values(), *row_copies.values(), *part_copies.values(), *spec_copies, *w_copies]:
        each.wait_send()


def body(n, ma, grad_fourier, legendre, spectra, filter_weight):
    orders, rows, _, chans = grad_fourier.shape
    deg = filter_weight.shape[0]
    dq = -(-deg // 8) * 8
    width = chans // ma
    cuts = max(2 * width // 128, 1)
    chunks = ma * cuts
    lanes = 2 * width // cuts
    blocks = n // GROUP
    flat_rows = grad_fourier.transpose(0, 2, 1, 3).reshape(2 * orders, rows, chans)
    spec = jnp.pad(spectra, ((0, dq - deg), (0, 0), (0, 0), (0, 0))).transpose(1, 2, 0, 3)
    spec = spec.reshape(ma, orders, 2 * dq, width)
    vmem = pl.BlockSpec(memory_space=pltpu.VMEM)
    dma = pltpu.SemaphoreType.DMA
    grads, wgrad = pl.pallas_call(
        functools.partial(kernel, (n, ma, orders, rows, deg, dq, chans, cuts)),
        out_shape=(
            jax.ShapeDtypeStruct((orders, 2, dq, chans), jnp.float32),
            jax.ShapeDtypeStruct((2, dq, width), jnp.float32),
        ),
        in_specs=[pl.BlockSpec(memory_space=pltpu.HBM), vmem, vmem],
        out_specs=(vmem, vmem),
        scratch_shapes=[
            pltpu.VMEM(legendre.shape, jnp.bfloat16),
            pltpu.VMEM((GROUP, blocks * dq, 2 * rows), jnp.bfloat16),
            pltpu.VMEM((GROUP, blocks * dq, 2 * rows), jnp.bfloat16),
            pltpu.VMEM((2 * blocks * dq, GROUP * rows), jnp.bfloat16),
            pltpu.VMEM((chunks, rows, lanes), jnp.bfloat16),
            pltpu.VMEM((chunks, GROUP, rows, lanes), jnp.bfloat16),
            pltpu.VMEM((chunks, 2 * blocks, dq, lanes), jnp.float32),
            pltpu.VMEM((chunks, blocks, 2, dq, lanes), jnp.float32),
            pltpu.VMEM((ma * orders, dq, 2 * width), jnp.float32),
            pltpu.VMEM((ma, orders, 2 * dq, width), jnp.bfloat16),
            pltpu.VMEM((ma, 2, dq, width), jnp.float32),
            pltpu.VMEM((ma, 2, dq, width), jnp.float32),
            dma(()),
            dma((GROUP,)), dma((GROUP,)),
            dma((chunks, GROUP)), dma((chunks, GROUP)),
            dma((chunks, blocks, 2)), dma((chunks, blocks, 2)),
            dma((ma,)), dma((ma,)),
            dma((ma,)), dma((ma,)),
        ],
        compiler_params=pltpu.CompilerParams(
            collective_id=0, has_side_effects=True, vmem_limit_bytes=24 * 1024 * 1024),
        cost_estimate=pl.CostEstimate(
            flops=4 * orders * blocks * dq * GROUP * rows * chans, bytes_accessed=8 * orders * dq * chans, transcendentals=0),
    )(legendre, flat_rows, spec)
    grads = grads[:, :, :deg].transpose(2, 0, 1, 3)
    real_grad = grads[:, :, 0, :]
    imag_grad = grads[:, :, 1, :]
    real_weight = filter_weight[:, None, 0, :]
    imag_weight = filter_weight[:, None, 1, :]
    input_grad = jnp.stack(
        [
            real_weight * real_grad + imag_weight * imag_grad,
            real_weight * imag_grad - imag_weight * real_grad,
        ],
        axis=2,
    )
    return input_grad, wgrad[:, :deg].transpose(1, 0, 2)


def solution(mesh):
    in_specs = (
        P("ma", "lat", None, None),
        P("ma", "lat", None),
        P("lat", None, None, "ma"),
        P("lat", None, None),
    )
    out_specs = (P("lat", "ma", None, None), P("lat", None, "ma"))
    fn = functools.partial(body, mesh.shape["lat"], mesh.shape["ma"])
    return jax.shard_map(fn, mesh=mesh, in_specs=in_specs, out_specs=out_specs, check_vma=False)
```
